32 devices in a mesh: snap: 2 (over y), pair: 4 (over z), ri: 4 (over x, core).
Axes of the slice: x: 2, y: 2, z: 4, core: 2. Of those that a mesh axis runs over, the one named last changes fastest.
Arguments:
- three_c: bfloat16 [32, 4, 64, 4096], P(('snap', 'pair'), 'ri'), parts along dimension 0, may hold values from -1.5 to 1.5
- green_occ: bfloat16 [32, 64, 64], P(('snap', 'pair')), parts along dimension 0, may hold values from -0.75 to 0.75
- green_virt: bfloat16 [32, 64, 64], P(('snap', 'pair')), parts along dimension 0, may hold values from -0.75 to 0.75
- pair_size: int32 [32], P(('snap', 'pair')), parts along dimension 0, may hold values from 16 to 64
- ri_ids: int32 [32, 4], P(('snap', 'pair')), parts along dimension 0, may hold values from 0 to 7, as said below
- coulomb: bfloat16 [1024, 512], P(('snap', 'pair', 'ri')), parts along dimension 0, may hold values from -0.25 to 0.25
Outputs:
- chi: float32 [1024, 512], P(('snap', 'pair', 'ri')), parts along dimension 0
- screen: float32 [1024, 512], P(('snap', 'pair', 'ri')), parts along dimension 0
The draws below stay inside these ranges and needn't reach their ends.
There are 2 independent parts, one for each index of `snap`. The reference program is written for one: setup_inputs(seed, part) draws one part's arguments, and reference() takes and returns one part's arrays. A program takes and returns all parts, laid end to end along the dimension named above; each array names one. Nothing has to cross between parts.
Inputs may be any that keep to these rules, and one draw needn't show every extreme that they name: `ri_ids`: each row names 4 different RI blocks.
All inputs are finite; a program needn't handle non-finite values.
Results may differ from the reference program's by a relative error of at most 0.005.
Values may be sent and summed in bfloat16 or wider, within the bound.
No kernel may reach another device: no remote copies, remote signals or barrier semaphores. Data moves between devices by JAX's collectives and lax.ppermute only.
A program may use at most 128 MiB of HBM per device.

```python
import jax
import jax.numpy as jnp
from jax import lax

AB = 64
RB = 64
KRI = 4
NPAIR = 16
NRIB = 8
NRI = 512


def draw_ri_ids(key, part):
    key = jax.random.fold_in(key, 7)
    keys = jax.random.split(key, NPAIR)

    def one_row(row_key):
        return jax.random.permutation(row_key, NRIB)[:KRI]
    return jax.vmap(one_row)(keys).astype(jnp.int32)


def with_ends(result, key, least, top_value):
    spot = [jax.random.randint(jax.random.fold_in(key, axis), (), 0, length) for axis, length in enumerate(result.shape)]
    longest = result.shape.index(max(result.shape))
    beside = spot[:longest] + [(spot[longest] + 1) % result.shape[longest]] + spot[longest + 1:]
    return result.at[tuple(spot)].set(least).at[tuple(beside)].set(top_value)


def block_scale(own_key, dims, shards, smallest, largest):
    loudness, own = 1.0, jax.random.fold_in(own_key, 6)
    for axis_at, blocks in shards:
        heights = jnp.exp(jax.random.uniform(jax.random.fold_in(own, axis_at), (blocks,), jnp.float32, smallest / len(shards), largest / len(shards)))
        loudness = loudness * jnp.repeat(heights, dims[axis_at] // blocks).reshape([-1 if axis == axis_at else 1 for axis in range(len(dims))])
    return loudness


def scatter_about(rng, dims, spread, limit, shards=(), kind=jnp.bfloat16):
    factor_of = block_scale(rng, dims, shards, -0.22, 0.18) if shards else 1.0
    entries = jax.random.normal(rng, dims, jnp.float32) * spread * factor_of
    return jnp.minimum(jnp.maximum(entries, -limit), limit).astype(kind)


def setup_inputs(seed: int = 0, part: int = 0) -> dict:
    key_list = jax.random.split(jax.random.key(seed), 7)
    part_keys = jax.random.split(jax.random.fold_in(key_list[6], part), 7)
    return {
        "three_c": scatter_about(part_keys[0], (NPAIR, KRI, RB, AB * AB), 0.1, 1.5, ((0, 4), (1, 4))),
        "green_occ": scatter_about(part_keys[1], (NPAIR, AB, AB), AB ** -0.5, 0.75, ((0, 4),)),
        "green_virt": scatter_about(part_keys[2], (NPAIR, AB, AB), AB ** -0.5, 0.75, ((0, 4),)),
        "pair_size": with_ends(jax.random.randint(part_keys[3], (NPAIR,), AB // 4, AB + 1), jax.random.fold_in(part_keys[3], 1), AB // 4, AB).astype(jnp.int32),
        "ri_ids": draw_ri_ids(jax.random.fold_in(jax.random.fold_in(key_list[6], part), 71), part),
        "coulomb": scatter_about(part_keys[5], (NRI, NRI), NRI ** -0.5, 0.25, ((0, 16),)),
    }


def products_ref(blocks, occ, virt, size):
    kcount, rows, square = blocks.shape
    width = occ.shape[-1]
    shaped = blocks.reshape(kcount, rows, width, width)
    keep = (jnp.arange(width, dtype=jnp.int32) < size).astype(blocks.dtype)
    masked = (shaped * keep[None, None, :, None]).astype(jnp.float32)
    left = jnp.einsum("krmn,nl->krml", masked, occ.astype(jnp.float32)).astype(jnp.bfloat16)
    right = jnp.einsum("ms,krsl->krml", virt.astype(jnp.float32), masked).astype(jnp.bfloat16)
    return left.reshape(kcount * rows, square), right.reshape(kcount * rows, square)


def reference(three_c, green_occ, green_virt, pair_size, ri_ids, coulomb):
    onehot = (ri_ids[:, :, None] == jnp.arange(NRIB, dtype=jnp.int32)[None, None, :]).astype(jnp.float32)

    def step(total, item):
        blocks, occ, virt, size, picks = item
        left, right = products_ref(blocks, occ, virt, size)
        pair_chi = jnp.dot(left.astype(jnp.float32), right.astype(jnp.float32).T, precision=lax.Precision.HIGHEST)
        pair_chi = pair_chi.reshape(KRI, RB, KRI, RB)
        half = jnp.einsum("kr,kalb->ralb", picks, pair_chi, precision=lax.Precision.HIGHEST)
        whole = jnp.einsum("ralb,lt->ratb", half, picks, precision=lax.Precision.HIGHEST)
        return total + whole.reshape(NRI, NRI), None

    start = jnp.zeros((NRI, NRI), jnp.float32)
    chi, _ = lax.scan(step, start, (three_c, green_occ, green_virt, pair_size, onehot))
    screen = jnp.dot(chi.astype(jnp.bfloat16), coulomb, preferred_element_type=jnp.float32)
    return chi, screen
```

```python
import jax
import jax.numpy as jnp
from jax import lax
from jax.sharding import PartitionSpec as P


def block_products(blocks, occ, virt, size):
    kcount, rows, square = blocks.shape
    width = occ.shape[-1]
    keep = lax.broadcasted_iota(jnp.int32, (width, width), 0) < size
    keep = (keep & (lax.broadcasted_iota(jnp.int32, (width, width), 1) < size)).astype(blocks.dtype)
    shaped = blocks.reshape(kcount, rows, width, width)
    left = jnp.einsum("krmn,nl->krml", shaped, occ, preferred_element_type=jnp.float32)
    right = jnp.einsum("ms,krsl->krml", virt * keep, shaped, preferred_element_type=jnp.float32)
    left = left.astype(jnp.bfloat16).reshape(kcount * rows, square)
    right = right.astype(jnp.bfloat16).reshape(kcount * rows, square)
    return left, right


def swap(array, axes, step):
    count = lax.axis_size(axes)
    return lax.ppermute(array, axes, [(i, i ^ step) for i in range(count)])


def shards(three_c, green_occ, green_virt, pair_size, ri_ids, coulomb):
    everyone = ("pair", "ri")
    ri_count = lax.axis_size("ri")
    devices = lax.axis_size(everyone)
    here = lax.axis_index("ri")
    kcount = ri_ids.shape[1]
    rows = three_c.shape[2]
    blocks_ri = 2 * kcount
    out_rows = coulomb.shape[0]

    own = lax.dynamic_index_in_dim(three_c, here, 0, keepdims=False)
    parts = [own]
    for step in range(1, ri_count):
        part = lax.dynamic_index_in_dim(three_c, here ^ step, 0, keepdims=False)
        parts.append(swap(part, "ri", step))
    pick = lambda array: lax.dynamic_index_in_dim(array, here, 0, keepdims=False)
    occ, virt, size, ids = pick(green_occ), pick(green_virt), pick(pair_size), pick(ri_ids)
    left, right = block_products(jnp.concatenate(parts, 0), occ, virt, size)
    chi = jnp.dot(left, right.T, preferred_element_type=jnp.float32)

    order = here ^ jnp.arange(kcount, dtype=jnp.int32)
    ids = ids[order]
    block_ids = jnp.arange(blocks_ri, dtype=jnp.int32)
    onehot = (ids[:, None] == block_ids[None, :]).astype(jnp.bfloat16)
    chi = chi.astype(jnp.bfloat16).reshape(kcount, rows, kcount * rows)
    spread = jnp.einsum("kr,kac->rac", onehot, chi).reshape(devices, out_rows, kcount * rows)
    got = lax.all_to_all(spread, everyone, 0, 0, tiled=True)
    all_ids = lax.all_gather(ids, everyone)
    onehots = (all_ids[:, :, None] == block_ids[None, None, :]).astype(jnp.float32)
    got = got.astype(jnp.float32).reshape(devices, out_rows, kcount, rows)
    chi_rows = jnp.einsum("drkq,dkt->rtq", got, onehots, precision=lax.Precision.HIGHEST)
    chi_rows = chi_rows.reshape(out_rows, blocks_ri * rows)
    metric = lax.all_gather(coulomb, everyone, axis=0, tiled=True)
    screen = jnp.dot(chi_rows.astype(jnp.bfloat16), metric, preferred_element_type=jnp.float32)
    return chi_rows, screen


def solution(mesh):
    placed = (
        P(("snap", "pair"), "ri", None, None),
        P(("snap", "pair"), None, None),
        P(("snap", "pair"), None, None),
        P(("snap", "pair")),
        P(("snap", "pair"), None),
        P(("snap", "pair", "ri"), None),
    )

    def inner(three_c, *rest):
        return shards(three_c[:, 0][:, None], *rest)

    return jax.shard_map(
        inner,
        mesh=mesh,
        in_specs=placed,
        out_specs=(P(("snap", "pair", "ri"), None), P(("snap", "pair", "ri"), None)),
        check_vma=False,
    )
```

```python
import functools

import jax
import jax.numpy as jnp
from jax import lax
from jax.experimental import pallas as pl
from jax.experimental.pallas import tpu as pltpu
from jax.sharding import PartitionSpec as P

LANES = 128
VMEM_LIMIT = 48 * 1024 * 1024


def iota(shape, dim):
    return lax.broadcasted_iota(jnp.int32, shape, dim)


def dot(a, b):
    return jnp.dot(a, b, preferred_element_type=jnp.float32)


def dot_nt(a, b):
    return lax.dot_general(a, b, (((1,), (1,)), ((), ())), preferred_element_type=jnp.float32)


def prep_kernel(scalars, occ, virt, occ_out, virt_out):
    size = scalars[1]
    width = occ.shape[1]
    half = width // 2
    full = occ_out.shape[0]
    one = lambda hit: jnp.where(hit, 1.0, 0.0)
    spread = one(iota((full, width), 0) % width == iota((full, width), 1)).astype(jnp.bfloat16)
    tiled = dot_nt(dot(spread, occ[0]).astype(jnp.bfloat16), spread)
    same = iota((full, full), 0) // width == iota((full, full), 1) // width
    occ_out[...] = jnp.where(same, tiled, 0.0).astype(jnp.bfloat16)

    keep = (iota((width, width), 0) < size) & (iota((width, width), 1) < size)
    kept = jnp.where(keep, virt[0].astype(jnp.float32), 0.0).astype(jnp.bfloat16)
    group = full // 2
    copies_row = iota((group, full), 0) // half
    copies_col = iota((group, full), 1) % group // half
    for parity in range(2):
        wanted = 2 * (iota((group, width), 0) % half) + parity
        picked_rows = one(wanted == iota((group, width), 1)).astype(jnp.bfloat16)
        column = iota((full, width), 0)
        side = column // group
        wanted = 2 * (column % half) + (side + parity) % 2
        picked_columns = one(wanted == iota((full, width), 1)).astype(jnp.bfloat16)
        part = dot_nt(dot(picked_rows, kept).astype(jnp.bfloat16), picked_columns)
        part = jnp.where(copies_row == copies_col, part, 0.0)
        virt_out[parity * group : (parity + 1) * group, :] = part.astype(jnp.bfloat16)


def prep(scalars, occ, virt):
    width = occ.shape[-1]
    full = 4 * width
    pick = pl.BlockSpec((1, width, width), lambda i, s: (s[0], 0, 0))
    whole = pl.BlockSpec((full, full), lambda i, s: (0, 0))
    return pl.pallas_call(
        prep_kernel,
        grid_spec=pltpu.PrefetchScalarGridSpec(
            num_scalar_prefetch=1, grid=(1,), in_specs=[pick, pick], out_specs=[whole, whole]
        ),
        out_shape=[jax.ShapeDtypeStruct((full, full), jnp.bfloat16)] * 2,
        name="prep",
    )(scalars, occ, virt)


def transform(block, occ, virt, left, right, spread, mixed):
    rows, square = block.shape
    full = occ.shape[0]
    group = full // 2
    chunks = square // LANES
    for c in range(square // full):
        at = slice(c * full, (c + 1) * full)
        left[:, at] = dot(block[:, at], occ[...]).astype(jnp.bfloat16)
    for c in range(chunks):
        piece = block[:, c * LANES : (c + 1) * LANES].astype(jnp.float32)
        spread[pl.ds(c, rows, stride=chunks), :] = piece
    low = iota((group, full), 1) % LANES < LANES // 2
    for g in range(0, rows * chunks, 2 * group):
        one, two = spread[g : g + group, :], spread[g + group : g + 2 * group, :]
        plain = jnp.concatenate([one, two], 1).astype(jnp.bfloat16)
        turned = jnp.concatenate(
            [pltpu.roll(one, LANES // 2, 1), pltpu.roll(two, LANES // 2, 1)], 1
        ).astype(jnp.bfloat16)
        out = dot(virt[...], jnp.concatenate([plain, turned], 0))
        out = jnp.where(low, out[:group], out[group:])
        mixed[g : g + group, :] = out[:, :LANES]
        mixed[g + group : g + 2 * group, :] = out[:, LANES:]
    for c in range(chunks):
        piece = mixed[pl.ds(c, rows, stride=chunks), :]
        right[:, c * LANES : (c + 1) * LANES] = piece.astype(jnp.bfloat16)


def transform_kernel(scalars, block, occ, virt, left, right, spread, mixed):
    transform(block.at[0], occ, virt, left, right, spread, mixed)


def transformed(scalars, blocks, occ, virt, picked):
    _, rows, square = blocks.shape
    full = occ.shape[0]
    where = (lambda i, s: (s[0], 0, 0)) if picked else (lambda i, s: (0, 0, 0))
    whole = pl.BlockSpec((full, full), lambda i, s: (0, 0))
    out = pl.BlockSpec((rows, square), lambda i, s: (0, 0))
    scratch = pltpu.VMEM((rows * (square // LANES), LANES), jnp.float32)
    return pl.pallas_call(
        transform_kernel,
        grid_spec=pltpu.PrefetchScalarGridSpec(
            num_scalar_prefetch=1,
            grid=(1,),
            in_specs=[pl.BlockSpec((1, rows, square), where), whole, whole],
            out_specs=[out, out],
            scratch_shapes=[scratch, scratch],
        ),
        out_shape=[jax.ShapeDtypeStruct((rows, square), jnp.bfloat16)] * 2,
        compiler_params=pltpu.CompilerParams(vmem_limit_bytes=VMEM_LIMIT),
        cost_estimate=pl.CostEstimate(
            flops=4 * rows * square * full, bytes_accessed=6 * rows * square, transcendentals=0
        ),
        name="transform",
    )(scalars, blocks, occ, virt)


def chi_kernel(count, ids, *refs):
    lefts, rights, out = refs[:count], refs[count : 2 * count], refs[2 * count]
    rows = lefts[0].shape[0]
    out[...] = jnp.zeros_like(out)
    for k in range(count):
        for half in range(0, count, 2):
            pair = [dot_nt(lefts[k][...], rights[half + i][...]) for i in range(2)]
            at = slice(half * rows, (half + 2) * rows)
            out[ids[k], :, at] = jnp.concatenate(pair, 1).astype(jnp.bfloat16)


def chi_pieces(ids, lefts, rights):
    count = len(lefts)
    rows, square = lefts[0].shape
    return pl.pallas_call(
        functools.partial(chi_kernel, count),
        in_specs=[pl.BlockSpec(memory_space=pltpu.SMEM)]
        + [pl.BlockSpec(memory_space=pltpu.VMEM)] * (2 * count),
        out_specs=pl.BlockSpec(memory_space=pltpu.VMEM),
        out_shape=jax.ShapeDtypeStruct((2 * count, rows, count * rows), jnp.bfloat16),
        compiler_params=pltpu.CompilerParams(vmem_limit_bytes=VMEM_LIMIT),
        name="pair_chi",
    )(ids, *lefts, *rights)


def finish_kernel(ri_count, ids, got, metric, chi, screen, even, odd):
    sources, rows, columns = got.shape
    kcount = ids.shape[1]
    width = columns // kcount
    even[...] = jnp.zeros_like(even)
    odd[...] = jnp.zeros_like(odd)

    def add(source_group, carry):
        for ri in range(ri_count):
            source = source_group * ri_count + ri
            for j in range(0, kcount, 2):
                piece = got[source, :, j * width : (j + 2) * width].astype(jnp.float32)
                even[ids[source, ri ^ j]] += piece
                odd[ids[source, ri ^ (j + 1)]] += piece
        return carry

    lax.fori_loop(0, sources // ri_count, add, 0)
    low = iota((rows, LANES), 1) < width
    for t in range(0, 2 * kcount, 2):
        first = even[t] + pltpu.roll(odd[t], width, 1)
        second = odd[t + 1] + pltpu.roll(even[t + 1], width, 1)
        chi[:, t * width : (t + 2) * width] = jnp.where(low, first, second)
    screen[...] = dot(chi[...].astype(jnp.bfloat16), metric[...])


def finish(ids, got, metric, ri_count):
    sources, rows, columns = got.shape
    total = metric.shape[0]
    blocks = 2 * ids.shape[1]
    scratch = pltpu.VMEM((blocks, rows, LANES), jnp.float32)
    vmem = pl.BlockSpec(memory_space=pltpu.VMEM)
    return pl.pallas_call(
        functools.partial(finish_kernel, ri_count),
        in_specs=[pl.BlockSpec(memory_space=pltpu.SMEM), vmem, vmem],
        out_specs=[vmem, vmem],
        out_shape=[jax.ShapeDtypeStruct((rows, total), jnp.float32)] * 2,
        scratch_shapes=[scratch, scratch],
        compiler_params=pltpu.CompilerParams(vmem_limit_bytes=VMEM_LIMIT),
        name="finish",
    )(ids, got, metric)


def swap(array, axes, step):
    count = lax.axis_size(axes)
    return lax.ppermute(array, axes, [(i, i ^ step) for i in range(count)])


def gathered(array, axis, step):
    other = swap(array, axis, step)
    upper = (lax.axis_index(axis) & step) != 0
    return jnp.where(upper, jnp.stack([other, array]), jnp.stack([array, other]))


def gather_metric(coulomb, ids):
    rows, total = coulomb.shape
    ri_count, pair_count = lax.axis_size("ri"), lax.axis_size("pair")
    out = coulomb[None]
    step = 2
    while step < ri_count:
        out = gathered(out, "ri", step).reshape(-1, rows, total)
        step *= 2
    step = 1
    all_ids = ids[None].astype(jnp.float32)
    while step < pair_count:
        out = gathered(out, "pair", step)
        out = out.reshape((-1,) + out.shape[2:])
        all_ids = gathered(all_ids, "pair", step).reshape((-1,) + all_ids.shape[1:])
        step *= 2
    out = gathered(out, "ri", 1)
    out = out.reshape(2, -1, rows, total).swapaxes(0, 1).reshape(-1, total)
    return out, all_ids.astype(jnp.int32).reshape(-1, ids.shape[-1])


def shards(three_c, green_occ, green_virt, pair_size, ri_ids, coulomb):
    everyone = ("pair", "ri")
    ri_count = lax.axis_size("ri")
    devices = lax.axis_size(everyone)
    here = lax.axis_index("ri")
    kcount = ri_ids.shape[1]
    pairs, _, rows, square = three_c.shape
    three_c = three_c.reshape(pairs, rows, square)

    parts = {}
    for step in list(range(2, ri_count)) + [1]:
        part = lax.dynamic_slice_in_dim(three_c, here ^ step, 1, 0)
        parts[step] = swap(part, "ri", step)
    metric, all_ids = gather_metric(coulomb, ri_ids)

    pick = lambda array: lax.dynamic_index_in_dim(array, here, 0, keepdims=False)
    scalars = jnp.stack([here, pick(pair_size)]).astype(jnp.int32)
    occ, virt = prep(scalars, green_occ, green_virt)
    lefts, rights = [], []
    for step in range(ri_count):
        left, right = transformed(scalars, parts.get(step, three_c), occ, virt, step == 0)
        lefts.append(left)
        rights.append(right)
    ids = pick(ri_ids)[here ^ jnp.arange(kcount, dtype=jnp.int32)]
    pieces = chi_pieces(ids, lefts, rights)
    pieces = pieces.reshape(devices, -1, kcount * rows)
    got = lax.all_to_all(pieces, everyone, 0, 0, tiled=True)
    return tuple(finish(all_ids, got, metric, ri_count))


def solution(mesh):
    placed = (
        P(("snap", "pair"), "ri", None, None),
        P(("snap", "pair"), None, None),
        P(("snap", "pair"), None, None),
        P(("snap", "pair")),
        P(("snap", "pair"), None),
        P(("snap", "pair", "ri"), None),
    )
    return jax.shard_map(
        shards,
        mesh=mesh,
        in_specs=placed,
        out_specs=(P(("snap", "pair", "ri"), None), P(("snap", "pair", "ri"), None)),
        check_vma=False,
    )
```

```python
import functools

import jax
import jax.numpy as jnp
from jax import lax
from jax.experimental import pallas as pl
from jax.experimental.pallas import tpu as pltpu
from jax.sharding import PartitionSpec as P

LANES = 128
SUB = 8
VMEM_LIMIT = 48 * 1024 * 1024


def iota(shape, dim):
    return lax.broadcasted_iota(jnp.int32, shape, dim)


def dot(a, b):
    return jnp.dot(a, b, preferred_element_type=jnp.float32)


def dot_nt(a, b):
    return lax.dot_general(a, b, (((1,), (1,)), ((), ())), preferred_element_type=jnp.float32)


def prepared(size, occ, virt, occ_out, virt_out):
    width = occ.shape[0]
    full = occ_out.shape[0]
    one = lambda hit: jnp.where(hit, 1.0, 0.0).astype(jnp.bfloat16)
    spread = one(iota((full, width), 0) % width == iota((full, width), 1))
    tiled = dot_nt(dot(spread, occ).astype(jnp.bfloat16), spread)
    same = iota((full, full), 0) // width == iota((full, full), 1) // width
    occ_out[...] = jnp.where(same, tiled, 0.0).astype(jnp.bfloat16)

    keep = (iota((width, width), 0) < size) & (iota((width, width), 1) < size)
    kept = jnp.where(keep, virt.astype(jnp.float32), 0.0).astype(jnp.bfloat16)
    half = virt_out.shape[0] // 2
    same = iota((half, 2 * half), 0) % SUB == iota((half, 2 * half), 1) % SUB
    for parity in range(2):
        wanted = 2 * (iota((half, width), 0) // SUB) + parity
        picked_rows = one(wanted == iota((half, width), 1))
        column = iota((2 * half, width), 0)
        wanted = 2 * (column % half // SUB) + (column // half + parity) % 2
        picked_columns = one(wanted == iota((2 * half, width), 1))
        part = dot_nt(dot(picked_rows, kept).astype(jnp.bfloat16), picked_columns)
        part = jnp.where(same, part, 0.0).astype(jnp.bfloat16)
        virt_out[parity * half : (parity + 1) * half, :] = part


def transform(block, occ, virt, left, right):
    rows, square = right.shape
    full = occ.shape[0]
    chunks = square // LANES
    half = chunks * SUB
    for c in range(square // full):
        at = slice(c * full, (c + 1) * full)
        left[:, at] = dot(block[:, at], occ[...]).astype(jnp.bfloat16)
    low = iota((half, 2 * LANES), 1) % LANES < LANES // 2
    for row in range(0, rows, 2 * SUB):
        tile = block[row : row + 2 * SUB, :square].astype(jnp.float32)
        plain, turned = [], []
        for i in range(2):
            part = tile[i * SUB : (i + 1) * SUB]
            stacked = jnp.concatenate(
                [part[:, c * LANES : (c + 1) * LANES] for c in range(chunks)], 0
            )
            plain.append(stacked)
            turned.append(pltpu.roll(stacked, LANES // 2, 1))
        operand = jnp.concatenate(
            [jnp.concatenate(plain, 1), jnp.concatenate(turned, 1)], 0
        ).astype(jnp.bfloat16)
        out = dot(virt[...], operand)
        out = jnp.where(low, out[:half], out[half:])
        for c in range(chunks):
            piece = out[c * SUB : (c + 1) * SUB]
            piece = jnp.concatenate([piece[:, :LANES], piece[:, LANES:]], 0)
            right[row : row + 2 * SUB, c * LANES : (c + 1) * LANES] = piece.astype(jnp.bfloat16)


def first_kernel(scalars, own, other, occ, virt, occ_out, virt_out, left, right):
    prepared(scalars[1], occ[0], virt[0], occ_out, virt_out)
    rows = own.shape[1]
    for i, block in enumerate((own, other)):
        at = slice(i * rows, (i + 1) * rows)
        transform(block.at[0], occ_out, virt_out, left.at[at], right.at[at])


def first_blocks(scalars, three_c, other, occ, virt):
    _, rows, square = three_c.shape
    width = occ.shape[-1]
    pick = lambda shape: pl.BlockSpec((1,) + shape, lambda i, s: (s[0], 0, 0))
    whole = lambda *shape: pl.BlockSpec(shape, lambda i, s: (0,) * len(shape))
    shapes = [(4 * width, 4 * width), (SUB * width, SUB * width), (2 * rows, square), (2 * rows, square)]
    return pl.pallas_call(
        first_kernel,
        grid_spec=pltpu.PrefetchScalarGridSpec(
            num_scalar_prefetch=1,
            grid=(1,),
            in_specs=[pick((rows, square)), whole(1, rows, square), pick((width, width)), pick((width, width))],
            out_specs=[whole(*shape) for shape in shapes],
        ),
        out_shape=[jax.ShapeDtypeStruct(shape, jnp.bfloat16) for shape in shapes],
        compiler_params=pltpu.CompilerParams(vmem_limit_bytes=VMEM_LIMIT),
        name="first_blocks",
    )(scalars, three_c, other, occ, virt)


def next_kernel(block, occ, virt, left, right):
    transform(block.at[0], occ, virt, left, right)


def next_block(block, occ, virt, square):
    rows = block.shape[1]
    vmem = pl.BlockSpec(memory_space=pltpu.VMEM)
    return pl.pallas_call(
        next_kernel,
        in_specs=[vmem] * 3,
        out_specs=[vmem] * 2,
        out_shape=[jax.ShapeDtypeStruct((rows, square), jnp.bfloat16)] * 2,
        compiler_params=pltpu.CompilerParams(vmem_limit_bytes=VMEM_LIMIT),
        name="next_block",
    )(block, occ, virt)


def last_kernel(count, ids, block, occ, virt, *refs):
    lefts, rights = list(refs[:count]), list(refs[count : 2 * count])
    out, left, right = refs[2 * count :]
    transform(block.at[0], occ, virt, left, right)
    lefts.append(left)
    rights.append(right)
    rows, square = left.shape
    step = 512
    total = None
    for c in range(0, square, step):
        a = jnp.concatenate([ref[:, c : c + step] for ref in lefts], 0)
        b = jnp.concatenate([ref[:, c : c + step] for ref in rights], 0)
        part = dot_nt(a, b)
        total = part if total is None else total + part
    out[...] = jnp.zeros_like(out)
    for k in range(total.shape[0] // rows):
        out[ids[k]] = total[k * rows : (k + 1) * rows].astype(jnp.bfloat16)


def last_block(ids, block, occ, virt, lefts, rights):
    count = ids.shape[0]
    _, rows, square = block.shape
    vmem = pl.BlockSpec(memory_space=pltpu.VMEM)
    scratch = pltpu.VMEM((rows, square), jnp.bfloat16)
    return pl.pallas_call(
        functools.partial(last_kernel, len(lefts)),
        in_specs=[pl.BlockSpec(memory_space=pltpu.SMEM)] + [vmem] * (3 + 2 * len(lefts)),
        out_specs=vmem,
        out_shape=jax.ShapeDtypeStruct((2 * count, rows, count * rows), jnp.bfloat16),
        scratch_shapes=[scratch, scratch],
        compiler_params=pltpu.CompilerParams(vmem_limit_bytes=VMEM_LIMIT),
        name="last_block",
    )(ids, block, occ, virt, *lefts, *rights)


def finish_kernel(ri_count, ids, got, metric, chi, screen, even, odd):
    sources, rows, columns = got.shape
    kcount = ids.shape[1]
    width = columns // kcount
    even[...] = jnp.zeros_like(even)
    odd[...] = jnp.zeros_like(odd)

    def add(source_group, carry):
        for ri in range(ri_count):
            source = source_group * ri_count + ri
            for j in range(0, kcount, 2):
                piece = got[source, :, j * width : (j + 2) * width].astype(jnp.float32)
                even[ids[source, ri ^ j]] += piece
                odd[ids[source, ri ^ (j + 1)]] += piece
        return carry

    lax.fori_loop(0, sources // ri_count, add, 0)
    low = iota((rows, LANES), 1) < width
    for t in range(0, 2 * kcount, 2):
        first = even[t] + pltpu.roll(odd[t], width, 1)
        second = odd[t + 1] + pltpu.roll(even[t + 1], width, 1)
        chi[:, t * width : (t + 2) * width] = jnp.where(low, first, second)
    screen[...] = dot(chi[...].astype(jnp.bfloat16), metric[...])


def finish(ids, got, metric, ri_count):
    sources, rows, columns = got.shape
    total = metric.shape[0]
    blocks = 2 * ids.shape[1]
    scratch = pltpu.VMEM((blocks, rows, LANES), jnp.float32)
    vmem = pl.BlockSpec(memory_space=pltpu.VMEM)
    return pl.pallas_call(
        functools.partial(finish_kernel, ri_count),
        in_specs=[pl.BlockSpec(memory_space=pltpu.SMEM), vmem, vmem],
        out_specs=[vmem, vmem],
        out_shape=[jax.ShapeDtypeStruct((rows, total), jnp.float32)] * 2,
        scratch_shapes=[scratch, scratch],
        compiler_params=pltpu.CompilerParams(vmem_limit_bytes=VMEM_LIMIT),
        name="finish",
    )(ids, got, metric)


def swap(array, axes, step):
    count = lax.axis_size(axes)
    return lax.ppermute(array, axes, [(i, i ^ step) for i in range(count)])


def gathered(array, axis, step):
    other = swap(array, axis, step)
    upper = (lax.axis_index(axis) & step) != 0
    return jnp.where(upper, jnp.stack([other, array]), jnp.stack([array, other]))


def folded(coulomb, rows):
    own_rows, total = coulomb.shape
    return jnp.concatenate(jnp.split(coulomb, rows // own_rows, 1), 0)


def gather_metric(coulomb, other, ids):
    rows, total = coulomb.shape
    ri_count, pair_count = lax.axis_size("ri"), lax.axis_size("pair")
    other = jnp.concatenate(jnp.split(other, other.shape[0] // rows, 0), 1)
    upper = (lax.axis_index("ri") & 2) != 0
    out = jnp.where(upper, jnp.stack([other, coulomb]), jnp.stack([coulomb, other]))
    step = 4
    while step < ri_count:
        out = gathered(out, "ri", step).reshape(-1, rows, total)
        step *= 2
    out = out.reshape(1, -1, total)
    count, kcount = ids.shape
    riding = jnp.pad(ids.astype(jnp.bfloat16), ((0, out.shape[1] - count), (0, LANES - kcount)))
    out = jnp.concatenate([out, riding[None]], 2)
    step = 1
    while step < pair_count:
        out = gathered(out, "pair", step)
        out = out.reshape((-1,) + out.shape[2:])
        step *= 2
    all_ids = out[:, :count, total : total + kcount].astype(jnp.int32).reshape(-1, kcount)
    out = gathered(out[:, :, :total], "ri", 1)
    out = out.reshape(2, -1, rows, total).swapaxes(0, 1).reshape(-1, total)
    return out, all_ids


def shards(three_c, green_occ, green_virt, pair_size, ri_ids, coulomb):
    everyone = ("pair", "ri")
    ri_count = lax.axis_size("ri")
    devices = lax.axis_size(everyone)
    here = lax.axis_index("ri")
    kcount = ri_ids.shape[1]
    pairs, _, rows, square = three_c.shape
    three_c = three_c.reshape(pairs, rows, square)

    parts = {}
    before = here
    for step in list(range(2, ri_count)) + [1]:
        part = lax.dynamic_slice_in_dim(three_c, before ^ step, 1, 0)
        if step == 2:
            part = jnp.concatenate([part, folded(coulomb, rows)[None]], 2)
        part, before = lax.optimization_barrier((part, here))
        parts[step] = swap(part, "ri", step)
    metric, all_ids = gather_metric(coulomb, parts[2][0, :, square:], ri_ids)

    pick = lambda array: lax.dynamic_index_in_dim(array, here, 0, keepdims=False)
    scalars = jnp.stack([here, pick(pair_size)]).astype(jnp.int32)
    ids = pick(ri_ids)[here ^ jnp.arange(kcount, dtype=jnp.int32)]
    occ, virt, left, right = first_blocks(scalars, three_c, parts[1], green_occ, green_virt)
    lefts, rights = [left], [right]
    for step in range(2, ri_count - 1):
        left, right = next_block(parts[step], occ, virt, square)
        lefts.append(left)
        rights.append(right)
    pieces = last_block(ids, parts[ri_count - 1], occ, virt, lefts, rights)
    pieces = pieces.reshape(devices, -1, kcount * rows)
    got = lax.all_to_all(pieces, everyone, 0, 0, tiled=True)
    return tuple(finish(all_ids, got, metric, ri_count))


def solution(mesh):
    placed = (
        P(("snap", "pair"), "ri", None, None),
        P(("snap", "pair"), None, None),
        P(("snap", "pair"), None, None),
        P(("snap", "pair")),
        P(("snap", "pair"), None),
        P(("snap", "pair", "ri"), None),
    )
    return jax.shard_map(
        shards,
        mesh=mesh,
        in_specs=placed,
        out_specs=(P(("snap", "pair", "ri"), None), P(("snap", "pair", "ri"), None)),
        check_vma=False,
    )
```

```python
import functools

import jax
import jax.numpy as jnp
from jax import lax
from jax.experimental import pallas as pl
from jax.experimental.pallas import tpu as pltpu
from jax.sharding import PartitionSpec as P

LANES = 128
SUB = 8
TOKEN = (16, 128)
VMEM_LIMIT = 20 * 1024 * 1024
SMALL_LIMIT = 4 * 1024 * 1024
VMEM = pl.BlockSpec(memory_space=pltpu.VMEM)
SMEM = pl.BlockSpec(memory_space=pltpu.SMEM)
ANY = pl.BlockSpec(memory_space=pl.ANY)


def iota(shape, dim):
    return lax.broadcasted_iota(jnp.int32, shape, dim)


def one(hit):
    return jnp.where(hit, 1.0, 0.0).astype(jnp.bfloat16)


def dot(a, b):
    return jnp.dot(a, b, preferred_element_type=jnp.float32)


def dot_nt(a, b):
    return lax.dot_general(a, b, (((1,), (1,)), ((), ())), preferred_element_type=jnp.float32)


def half(shape):
    return jax.ShapeDtypeStruct(shape, jnp.bfloat16)


def far(shape):
    return pltpu.HBM(shape, jnp.bfloat16)


def near(shape):
    return pltpu.VMEM(shape, jnp.bfloat16)


def in_near(array):
    return pltpu.with_memory_space_constraint(array, pltpu.VMEM)


def in_far(array):
    return pltpu.with_memory_space_constraint(array, pltpu.HBM)


def started(sems, pairs):
    copies = [pltpu.make_async_copy(a, b, sems.at[i]) for i, (a, b) in enumerate(pairs)]
    for copy in copies:
        copy.start()
    return copies


def finished(copies):
    for copy in copies:
        copy.wait()


def limit(size):
    return pltpu.CompilerParams(vmem_limit_bytes=size)


def pick_kernel(step, first, riding, pieces, *refs):
    three_c = refs[0]
    out, token, held, sems_in, sems_out = refs[-5:]
    token[...] = jnp.zeros_like(token)
    count, _ = held.shape
    square = three_c.shape[2]
    here = lax.axis_index("ri")
    step_rows = count // pieces
    pairs_in, pairs_out = [], []
    if riding:
        coulomb = refs[1]
        rows, total = coulomb.shape
        fold = count // rows
        wide = total // fold
        for i in range(fold):
            there = held.at[pl.ds(i * rows, rows), pl.ds(square, wide)]
            pairs_in.append((coulomb.at[:, pl.ds(i * wide, wide)], there))
    rides = len(pairs_in)
    for i in range(pieces):
        at = pl.ds(i * step_rows, step_rows)
        source = three_c.at[here ^ step, pl.ds(first + i * step_rows, step_rows)]
        pairs_in.append((source, held.at[at, pl.ds(0, square)]))
        pairs_out.append((held.at[at], out.at[0, at]))
    copies = started(sems_in, pairs_in)
    finished(copies[:rides])
    going = []
    for i, (a, b) in enumerate(pairs_out):
        copies[rides + i].wait()
        copy = pltpu.make_async_copy(a, b, sems_out.at[i])
        copy.start()
        going.append(copy)
    finished(going)


def pick(three_c, step, first, count, coulomb=None, hold=None):
    square = three_c.shape[2]
    riding = coulomb is not None
    operands = [in_far(three_c)] + [in_far(a) for a in (coulomb,) if a is not None] + [a for a in (hold,) if a is not None]
    extra = coulomb.size // count if riding else 0
    rides = count // coulomb.shape[0] if riding else 0
    pieces = count // 16
    return pl.pallas_call(
        functools.partial(pick_kernel, step, first, riding, pieces),
        in_specs=[ANY] * (len(operands) - (hold is not None)) + [VMEM] * (hold is not None),
        out_specs=[ANY, VMEM],
        out_shape=[far((1, count, square + extra)), half(TOKEN)],
        scratch_shapes=[
            pltpu.VMEM((count, square + extra), jnp.bfloat16),
            pltpu.SemaphoreType.DMA((rides + pieces,)),
            pltpu.SemaphoreType.DMA((pieces,)),
        ],
        compiler_params=limit(SMALL_LIMIT),
        name="pick",
    )(*operands)


def along_x_kernel(block, coulomb, ids, hold, out):
    rows, total = coulomb.shape
    upper = (lax.axis_index("ri") & 2) != 0
    own = coulomb[...]
    fold = block.shape[1] // rows
    tail = block[0]
    other = jnp.concatenate([tail[i * rows : (i + 1) * rows] for i in range(fold)], 1)
    out[0, :rows, :total] = jnp.where(upper, other, own)
    out[0, rows:, :total] = jnp.where(upper, own, other)
    out[0, :, total:] = ids[...]


def rows_along_x(block, coulomb, ids, hold):
    rows, total = coulomb.shape
    return pl.pallas_call(
        along_x_kernel,
        in_specs=[VMEM] * 4,
        out_specs=VMEM,
        out_shape=half((1, 2 * rows, total + LANES)),
        compiler_params=limit(SMALL_LIMIT),
        name="rows_along_x",
    )(block, coulomb, ids, hold)


def prepared(size, occ, virt, occ_out, virt_out):
    width = occ.shape[0]
    full = occ_out.shape[0]
    spread = one(iota((full, width), 0) % width == iota((full, width), 1))
    tiled = dot_nt(dot(spread, occ).astype(jnp.bfloat16), spread)
    same = iota((full, full), 0) // width == iota((full, full), 1) // width
    occ_out[...] = jnp.where(same, tiled, 0.0).astype(jnp.bfloat16)

    keep = (iota((width, width), 0) < size) & (iota((width, width), 1) < size)
    kept = jnp.where(keep, virt.astype(jnp.float32), 0.0).astype(jnp.bfloat16)
    side = virt_out.shape[0] // 2
    same = iota((side, 2 * side), 0) % SUB == iota((side, 2 * side), 1) % SUB
    for parity in range(2):
        wanted = 2 * (iota((side, width), 0) // SUB) + parity
        picked_rows = one(wanted == iota((side, width), 1))
        column = iota((2 * side, width), 0)
        wanted = 2 * (column % side // SUB) + (column // side + parity) % 2
        picked_columns = one(wanted == iota((2 * side, width), 1))
        part = dot_nt(dot(picked_rows, kept).astype(jnp.bfloat16), picked_columns)
        virt_out[parity * side : (parity + 1) * side, :] = jnp.where(same, part, 0.0).astype(jnp.bfloat16)


def transform(block, occ, virt, left, right):
    rows, square = right.shape
    full = occ.shape[0]
    chunks = square // LANES
    side = chunks * SUB
    wide = [block[:, c * full : (c + 1) * full] for c in range(square // full)]
    out = dot(jnp.concatenate(wide, 0), occ[...]).astype(jnp.bfloat16)
    for c in range(square // full):
        left[:, c * full : (c + 1) * full] = out[c * rows : (c + 1) * rows]
    low = iota((side, 2 * LANES), 1) % LANES < LANES // 2
    for row in range(0, rows, 2 * SUB):
        tile = block[row : row + 2 * SUB, :square].astype(jnp.float32)
        plain, turned = [], []
        for i in range(2):
            part = tile[i * SUB : (i + 1) * SUB]
            stacked = jnp.concatenate([part[:, c * LANES : (c + 1) * LANES] for c in range(chunks)], 0)
            plain.append(stacked)
            turned.append(pltpu.roll(stacked, LANES // 2, 1))
        operand = jnp.concatenate([jnp.concatenate(plain, 1), jnp.concatenate(turned, 1)], 0)
        out = dot(virt[...], operand.astype(jnp.bfloat16))
        out = jnp.where(low, out[:side], out[side:])
        for c in range(chunks):
            piece = out[c * SUB : (c + 1) * SUB]
            piece = jnp.concatenate([piece[:, :LANES], piece[:, LANES:]], 0)
            right[row : row + 2 * SUB, c * LANES : (c + 1) * LANES] = piece.astype(jnp.bfloat16)


def first_kernel(sizes, ids, three_c, other, occ, virt, *refs):
    occ_out, virt_out, left, right, place_out, token, own, place, sem, sems = refs
    token[...] = jnp.zeros_like(token)
    here = lax.axis_index("ri")
    copy = pltpu.make_async_copy(three_c.at[here], own, sem)
    copy.start()
    prepared(sizes[here], occ[here], virt[here], occ_out, virt_out)
    rows, square = own.shape
    column = iota(place.shape, 1)
    wanted = jnp.zeros(place.shape, jnp.int32)
    for j in range(ids.shape[1]):
        wanted = jnp.where(column // rows == j, ids[here, here ^ j], wanted)
    row = iota(place.shape, 0)
    place[...] = one((row // rows == wanted) & (row % rows == column % rows))
    copies = started(sems, [(place, place_out)])
    copy.wait()
    for i, block in enumerate((own, other.at[0])):
        at = slice(i * rows, (i + 1) * rows)
        transform(block, occ_out, virt_out, left.at[at], right.at[at])
    finished(copies)


def first_blocks(three_c, other, occ, virt, sizes, ids):
    _, rows, square = three_c.shape
    width = occ.shape[-1]
    kcount = ids.shape[1]
    shapes = [(4 * width, 4 * width), (SUB * width, SUB * width)] + [(2 * rows, square)] * 2
    place = (2 * kcount * rows, kcount * rows)
    return pl.pallas_call(
        first_kernel,
        in_specs=[SMEM, SMEM, ANY, VMEM, VMEM, VMEM],
        out_specs=[VMEM] * 4 + [ANY, VMEM],
        out_shape=[near(shape) for shape in shapes] + [far(place), half(TOKEN)],
        scratch_shapes=[
            pltpu.VMEM((rows, square), jnp.bfloat16),
            pltpu.VMEM(place, jnp.bfloat16),
            pltpu.SemaphoreType.DMA,
            pltpu.SemaphoreType.DMA((1,)),
        ],
        compiler_params=limit(VMEM_LIMIT),
        name="first_blocks",
    )(sizes, ids, in_far(three_c), other, occ, virt)


def next_kernel(block, occ, virt, hold, left_out, right_out, token, left, right, sems):
    token[...] = jnp.zeros_like(token)
    transform(block.at[0], occ, virt, left, right)
    finished(started(sems, [(left, left_out), (right, right_out)]))


def next_block(block, occ, virt, hold, square):
    shape = (block.shape[1], square)
    return pl.pallas_call(
        next_kernel,
        in_specs=[VMEM] * 4,
        out_specs=[ANY, ANY, VMEM],
        out_shape=[far(shape), far(shape), half(TOKEN)],
        scratch_shapes=[pltpu.VMEM(shape, jnp.bfloat16)] * 2 + [pltpu.SemaphoreType.DMA((2,))],
        compiler_params=limit(VMEM_LIMIT),
        name="next_block",
    )(block, in_near(occ), in_near(virt), hold)


def last_kernel(count, block, occ, virt, left_first, right_first, place_far, *refs):
    out, left, right, place, sems = refs[2 * count :]
    pairs, row = [], 0
    for i in range(count):
        at = pl.ds(row, refs[i].shape[0])
        pairs += [(refs[i], left.at[at]), (refs[count + i], right.at[at])]
        row += refs[i].shape[0]
    copies = started(sems, pairs + [(place_far, place)])
    transform(block.at[0], occ, virt, left.at[row:], right.at[row:])
    finished(copies)
    square = left.shape[1]
    step = 1024
    total = None
    for c in range(0, square, step):
        a = jnp.concatenate([ref[:, c : c + step] for ref in (left_first, left)], 0)
        b = jnp.concatenate([ref[:, c : c + step] for ref in (right_first, right)], 0)
        part = dot_nt(a, b)
        total = part if total is None else total + part
    out[...] = dot(place[...], total.astype(jnp.bfloat16)).astype(jnp.bfloat16)


def last_block(block, occ, virt, place, lefts, rights):
    _, rows, square = block.shape
    count = len(lefts) - 1
    rest = (place.shape[1] - lefts[0].shape[0], square)
    scratch = [pltpu.VMEM(shape, jnp.bfloat16) for shape in (rest, rest, place.shape)]
    return pl.pallas_call(
        functools.partial(last_kernel, count),
        in_specs=[VMEM] * 5 + [ANY] * (1 + 2 * count),
        out_specs=VMEM,
        out_shape=half(place.shape),
        scratch_shapes=scratch + [pltpu.SemaphoreType.DMA((1 + 2 * count,))],
        compiler_params=limit(VMEM_LIMIT),
        name="last_block",
    )(block, *map(in_near, (occ, virt, lefts[0], rights[0])), *map(in_far, [place] + lefts[1:] + rights[1:]))


def finish_kernel(kcount, place, got, metric, chi, screen):
    rows, total = chi.shape
    blocks = 2 * kcount
    width = total // blocks
    placed = dot(place[...], got[...])
    low = iota((rows, LANES), 1) < width

    def block(t):
        straight, turned = None, None
        for j in range(kcount):
            at = (j * blocks + t) * rows
            piece = placed[at : at + rows, j // 2 * LANES : (j // 2 + 1) * LANES]
            if j % 2 == t % 2:
                straight = piece if straight is None else straight + piece
            else:
                turned = piece if turned is None else turned + piece
        return straight + pltpu.roll(turned, width, 1)

    for t in range(0, blocks, 2):
        chi[:, t * width : (t + 2) * width] = jnp.where(low, block(t), block(t + 1))
    screen[...] = dot(chi[...].astype(jnp.bfloat16), metric[...])


def finish(place, got, metric, kcount):
    total = metric.shape[0]
    rows = place.shape[0] // (2 * kcount * kcount)
    return pl.pallas_call(
        functools.partial(finish_kernel, kcount),
        in_specs=[VMEM] * 3,
        out_specs=[VMEM, VMEM],
        out_shape=[jax.ShapeDtypeStruct((rows, total), jnp.float32)] * 2,
        compiler_params=limit(VMEM_LIMIT),
        name="finish",
    )(place, got, metric)


def placing_kernel(hits, out):
    high, wide = hits.shape
    rows = out.shape[0] // high
    down = one(iota((high * rows, high), 0) // rows == iota((high * rows, high), 1))
    across = one(iota((wide * rows, wide), 0) // rows == iota((wide * rows, wide), 1))
    spread = dot_nt(dot(down, hits[...]).astype(jnp.bfloat16), across)
    same = iota(out.shape, 0) % rows == iota(out.shape, 1) % rows
    out[...] = jnp.where(same, spread, 0.0).astype(jnp.bfloat16)


def placing(hits, rows):
    return pl.pallas_call(
        placing_kernel,
        in_specs=[VMEM],
        out_specs=VMEM,
        out_shape=half((hits.shape[0] * rows, hits.shape[1] * rows)),
        compiler_params=limit(VMEM_LIMIT),
        name="placing",
    )(hits)


def swap(array, axes, step):
    count = lax.axis_size(axes)
    return lax.ppermute(array, axes, [(i, i ^ step) for i in range(count)])


def gathered(array, axis, step):
    other = swap(array, axis, step)
    upper = (lax.axis_index(axis) & step) != 0
    return jnp.where(upper, jnp.stack([other, array]), jnp.stack([array, other]))


def gather_metric(out, total, own_rows, pairs, kcount):
    ri_count, pair_count = lax.axis_size("ri"), lax.axis_size("pair")
    chips = ri_count // 4
    _, rows, wide = out.shape
    step = 4
    while step < ri_count:
        out = gathered(out, "ri", step).reshape(-1, rows, wide)
        step *= 2
    step = 1
    while step < pair_count:
        out = gathered(out, "pair", step).reshape(-1, rows, wide)
        step *= 2
    all_ids = out.reshape(pair_count, chips, rows, wide)[:, 0, :pairs, total : total + kcount]
    out = out[:, :, :total].reshape(-1, rows // 2, total)[:, :own_rows]
    out = gathered(out, "ri", 1).swapaxes(0, 1).reshape(-1, total)
    return out, all_ids.reshape(-1, kcount)


def shards(three_c, green_occ, green_virt, pair_size, ri_ids, coulomb):
    everyone = ("pair", "ri")
    ri_count = lax.axis_size("ri")
    devices = lax.axis_size(everyone)
    kcount = ri_ids.shape[1]
    blocks = 2 * kcount
    pairs, _, rows, square = three_c.shape
    out_rows, total = coulomb.shape
    three_c = three_c.reshape(pairs, rows, square)
    slots = jnp.arange(kcount, dtype=jnp.int32)
    block_ids = jnp.arange(blocks, dtype=jnp.int32)
    riding_rows = max(16, out_rows)
    riding = jnp.pad(coulomb, ((0, riding_rows - out_rows), (0, 0)))

    parts, token = {}, None
    for step in list(range(2, ri_count)) + [1]:
        part, token = pick(three_c, step, 0, rows, coulomb=riding if step == 2 else None, hold=token)
        parts[step] = swap(part, "ri", step)
    occ, virt, left, right, place, token = first_blocks(
        three_c, parts[1], green_occ, green_virt, pair_size, ri_ids
    )
    lefts, rights, held = [left], [right], []
    for step in range(2, ri_count - 1):
        left, right, token = next_block(parts[step], occ, virt, token, square)
        lefts.append(left)
        rights.append(right)
        held.append(token)
    pieces = last_block(parts[ri_count - 1], occ, virt, place, lefts, rights)

    slot = jnp.arange(pairs, dtype=jnp.int32)[:, None] ^ slots[None, :]
    relative = jnp.sum(jnp.where(slot[:, :, None] == slots, ri_ids[:, None, :], 0), 2)
    ids = jnp.pad(relative.astype(jnp.bfloat16), ((0, 2 * riding_rows - pairs), (0, LANES - kcount)))
    metric = rows_along_x(parts[2][:, :, square:], riding, ids, held[0])
    metric, all_ids = gather_metric(metric, total, out_rows, pairs, kcount)
    hits = all_ids.T[:, None, :] == block_ids.astype(jnp.bfloat16)[None, :, None]
    placed = placing(hits.astype(jnp.bfloat16).reshape(kcount * blocks, devices), out_rows)

    got = lax.all_to_all(pieces.reshape(devices, out_rows, kcount * rows), everyone, 0, 0, tiled=True)
    return tuple(finish(placed, got.reshape(devices * out_rows, kcount * rows), metric, kcount))


def solution(mesh):
    placed = (
        P(("snap", "pair"), "ri", None, None),
        P(("snap", "pair"), None, None),
        P(("snap", "pair"), None, None),
        P(("snap", "pair")),
        P(("snap", "pair"), None),
        P(("snap", "pair", "ri"), None),
    )
    return jax.shard_map(
        shards,
        mesh=mesh,
        in_specs=placed,
        out_specs=(P(("snap", "pair", "ri"), None), P(("snap", "pair", "ri"), None)),
        check_vma=False,
    )
```

```python
import functools

import jax
import jax.numpy as jnp
from jax import lax
from jax.experimental import pallas as pl
from jax.experimental.pallas import tpu as pltpu
from jax.sharding import PartitionSpec as P

LANES = 128
SUB = 8
TOKEN = (16, 128)
VMEM_LIMIT = 20 * 1024 * 1024
SMALL_LIMIT = 4 * 1024 * 1024
VMEM = pl.BlockSpec(memory_space=pltpu.VMEM)
SMEM = pl.BlockSpec(memory_space=pltpu.SMEM)
ANY = pl.BlockSpec(memory_space=pl.ANY)


def iota(shape, dim):
    return lax.broadcasted_iota(jnp.int32, shape, dim)


def one(hit):
    return jnp.where(hit, 1.0, 0.0).astype(jnp.bfloat16)


def dot(a, b):
    return jnp.dot(a, b, preferred_element_type=jnp.float32)


def dot_nt(a, b):
    return lax.dot_general(a, b, (((1,), (1,)), ((), ())), preferred_element_type=jnp.float32)


def half(shape):
    return jax.ShapeDtypeStruct(shape, jnp.bfloat16)


def far(shape):
    return pltpu.HBM(shape, jnp.bfloat16)


def near(shape):
    return pltpu.VMEM(shape, jnp.bfloat16)


def in_near(array):
    return pltpu.with_memory_space_constraint(array, pltpu.VMEM)


def in_far(array):
    return pltpu.with_memory_space_constraint(array, pltpu.HBM)


def started(sems, pairs):
    copies = [pltpu.make_async_copy(a, b, sems.at[i]) for i, (a, b) in enumerate(pairs)]
    for copy in copies:
        copy.start()
    return copies


def finished(copies):
    for copy in copies:
        copy.wait()


def limit(size):
    return pltpu.CompilerParams(vmem_limit_bytes=size)


def pick_kernel(step, riding, *refs):
    three_c = refs[0]
    out, token, sems = refs[-3:]
    token[...] = jnp.zeros_like(token)
    _, count, _ = out.shape
    square = three_c.shape[2]
    pairs = [(three_c.at[lax.axis_index("ri") ^ step], out.at[0, :, pl.ds(0, square)])]
    if riding:
        coulomb = refs[1]
        rows, total = coulomb.shape
        fold = count // rows
        wide = total // fold
        for i in range(fold):
            there = out.at[0, pl.ds(i * rows, rows), pl.ds(square, wide)]
            pairs.append((coulomb.at[:, pl.ds(i * wide, wide)], there))
    finished(started(sems, pairs))


def pick(three_c, step, coulomb=None, hold=None):
    _, count, square = three_c.shape
    riding = coulomb is not None
    operands = [in_far(three_c)] + [in_far(a) for a in (coulomb,) if riding] + [a for a in (hold,) if a is not None]
    extra = coulomb.size // count if riding else 0
    rides = count // coulomb.shape[0] if riding else 0
    return pl.pallas_call(
        functools.partial(pick_kernel, step, riding),
        in_specs=[ANY] * (1 + riding) + [VMEM] * (hold is not None),
        out_specs=[VMEM, VMEM],
        out_shape=[near((1, count, square + extra)), half(TOKEN)],
        scratch_shapes=[pltpu.SemaphoreType.DMA((1 + rides,))],
        compiler_params=limit(SMALL_LIMIT),
        name="pick",
    )(*operands)


def along_x_kernel(block, coulomb, ids, hold, out):
    rows, total = coulomb.shape
    upper = (lax.axis_index("ri") & 2) != 0
    own = coulomb[...]
    fold = block.shape[1] // rows
    tail = block[0, :, block.shape[2] - total // fold :]
    other = jnp.concatenate([tail[i * rows : (i + 1) * rows] for i in range(fold)], 1)
    out[0, :rows, :total] = jnp.where(upper, other, own)
    out[0, rows:, :total] = jnp.where(upper, own, other)
    out[0, :, total:] = ids[...]


def rows_along_x(block, coulomb, ids, hold):
    rows, total = coulomb.shape
    return pl.pallas_call(
        along_x_kernel,
        in_specs=[VMEM] * 4,
        out_specs=VMEM,
        out_shape=half((1, 2 * rows, total + LANES)),
        compiler_params=limit(SMALL_LIMIT),
        name="rows_along_x",
    )(block, coulomb, ids, hold)


def prepared(size, occ, virt, occ_out, virt_out, back_out=None):
    width = occ.shape[0]
    full = occ_out.shape[0]
    spread = one(iota((full, width), 0) % width == iota((full, width), 1))
    tiled = dot_nt(dot(spread, occ).astype(jnp.bfloat16), spread)
    same = iota((full, full), 0) // width == iota((full, full), 1) // width
    occ_out[...] = jnp.where(same, tiled, 0.0).astype(jnp.bfloat16)

    keep = (iota((width, width), 0) < size) & (iota((width, width), 1) < size)
    kept = jnp.where(keep, virt.astype(jnp.float32), 0.0).astype(jnp.bfloat16)
    side = virt_out.shape[0] // 2
    same = iota((side, 2 * side), 0) % SUB == iota((side, 2 * side), 1) % SUB
    for parity in range(2):
        wanted = 2 * (iota((side, width), 0) // SUB) + parity
        picked_rows = one(wanted == iota((side, width), 1))
        column = iota((2 * side, width), 0)
        wanted = 2 * (column % side // SUB) + (column // side + parity) % 2
        picked_columns = one(wanted == iota((2 * side, width), 1))
        for target, product in ((virt_out, dot), (back_out, dot_nt)):
            if target is not None:
                part = dot_nt(product(picked_rows, kept).astype(jnp.bfloat16), picked_columns)
                target[parity * side : (parity + 1) * side, :] = jnp.where(same, part, 0.0).astype(jnp.bfloat16)


def times_occ(block, occ, left, product=dot):
    rows, square = left.shape
    full = occ.shape[0]
    wide = [block[:, c * full : (c + 1) * full] for c in range(square // full)]
    out = product(jnp.concatenate(wide, 0), occ[...]).astype(jnp.bfloat16)
    for c in range(square // full):
        left[:, c * full : (c + 1) * full] = out[c * rows : (c + 1) * rows]


def times_virt(virt, block, right):
    rows, square = right.shape
    chunks = square // LANES
    side = chunks * SUB
    low = iota((side, 2 * LANES), 1) % LANES < LANES // 2
    for row in range(0, rows, 2 * SUB):
        tile = block[row : row + 2 * SUB, :square].astype(jnp.float32)
        plain, turned = [], []
        for i in range(2):
            part = tile[i * SUB : (i + 1) * SUB]
            stacked = jnp.concatenate([part[:, c * LANES : (c + 1) * LANES] for c in range(chunks)], 0)
            plain.append(stacked)
            turned.append(pltpu.roll(stacked, LANES // 2, 1))
        operand = jnp.concatenate([jnp.concatenate(plain, 1), jnp.concatenate(turned, 1)], 0)
        out = dot(virt[...], operand.astype(jnp.bfloat16))
        out = jnp.where(low, out[:side], out[side:])
        for c in range(chunks):
            piece = out[c * SUB : (c + 1) * SUB]
            piece = jnp.concatenate([piece[:, :LANES], piece[:, LANES:]], 0)
            right[row : row + 2 * SUB, c * LANES : (c + 1) * LANES] = piece.astype(jnp.bfloat16)


def long_dot(lefts, rights, pad=0):
    square = lefts[0].shape[1]
    step = 1024
    total = None
    for c in range(0, square, step):
        a = jnp.concatenate([ref[:, c : c + step] for ref in lefts], 0)
        b = [ref[:, c : c + step] for ref in rights]
        zeros = [jnp.zeros((abs(pad), step), jnp.bfloat16)] if pad else []
        b = jnp.concatenate(b + zeros if pad > 0 else zeros + b, 0)
        part = dot_nt(a, b)
        total = part if total is None else total + part
    return total


def corner_kernel(step, sizes, three_c, occ, virt, hold, out, token, occ_wide, virt_wide, left, right, sem):
    token[...] = jnp.zeros_like(token)
    there = lax.axis_index("ri") ^ step
    rows, square = left.shape
    block = out.at[0, :, pl.ds(0, square)]
    copy = pltpu.make_async_copy(three_c.at[there], block, sem)
    copy.start()
    prepared(sizes[there], occ[there], virt[there], occ_wide, virt_wide)
    copy.wait()
    times_occ(block, occ_wide, left)
    times_virt(virt_wide, block, right)
    out[0, :, square:] = long_dot([left], [right], -rows).astype(jnp.bfloat16)


def corner(three_c, step, occ, virt, sizes, hold):
    _, rows, square = three_c.shape
    width = occ.shape[-1]
    shapes = [(4 * width, 4 * width), (SUB * width, SUB * width), (rows, square), (rows, square)]
    return pl.pallas_call(
        functools.partial(corner_kernel, step),
        in_specs=[SMEM, ANY, VMEM, VMEM, VMEM],
        out_specs=[VMEM, VMEM],
        out_shape=[near((1, rows, square + 2 * rows)), half(TOKEN)],
        scratch_shapes=[pltpu.VMEM(shape, jnp.bfloat16) for shape in shapes] + [pltpu.SemaphoreType.DMA],
        compiler_params=limit(VMEM_LIMIT),
        name="corner",
    )(sizes, in_far(three_c), occ, virt, hold)


def first_kernel(sizes, ids, three_c, other, occ, virt, hold, *refs):
    occ_out, virt_out, back_out, place, left, right, left_back, right_back, token, own, sem = refs
    token[...] = jnp.zeros_like(token)
    here = lax.axis_index("ri")
    copy = pltpu.make_async_copy(three_c.at[here], own, sem)
    copy.start()
    prepared(sizes[here], occ[here], virt[here], occ_out, virt_out, back_out)
    rows, square = own.shape
    column = iota(place.shape, 1)
    wanted = jnp.zeros(place.shape, jnp.int32)
    for j in range(ids.shape[1]):
        wanted = jnp.where(column // rows == j, ids[here, here ^ j], wanted)
    row = iota(place.shape, 0)
    place[...] = one((row // rows == wanted) & (row % rows == column % rows))
    copy.wait()
    for i, block in enumerate((own, other.at[0])):
        at = slice(i * rows, (i + 1) * rows)
        times_occ(block, occ_out, left.at[at])
        times_virt(virt_out, block, right.at[at])
        times_virt(back_out, left.at[at], left_back.at[at])
        times_occ(right.at[at], occ_out, right_back.at[at], dot_nt)


def first_blocks(three_c, other, occ, virt, sizes, ids, hold):
    _, rows, square = three_c.shape
    width = occ.shape[-1]
    kcount = ids.shape[1]
    shapes = [(4 * width, 4 * width)] + [(SUB * width, SUB * width)] * 2
    shapes += [(2 * kcount * rows, kcount * rows)] + [(2 * rows, square)] * 4
    return pl.pallas_call(
        first_kernel,
        in_specs=[SMEM, SMEM, ANY] + [VMEM] * 4,
        out_specs=[VMEM] * 9,
        out_shape=[near(shape) for shape in shapes] + [half(TOKEN)],
        scratch_shapes=[pltpu.VMEM((rows, square), jnp.bfloat16), pltpu.SemaphoreType.DMA],
        compiler_params=limit(VMEM_LIMIT),
        name="first_blocks",
    )(sizes, ids, in_far(three_c), other, occ, virt, hold)


def next_kernel(block, occ, virt, virt_back, hold, left, right, left_back, right_back, token):
    token[...] = jnp.zeros_like(token)
    times_occ(block.at[0], occ, left)
    times_virt(virt, block.at[0], right)
    times_virt(virt_back, left, left_back)
    times_occ(right, occ, right_back, dot_nt)


def next_block(block, occ, virt, virt_back, hold, square):
    shape = (block.shape[1], square)
    return pl.pallas_call(
        next_kernel,
        in_specs=[VMEM] * 5,
        out_specs=[VMEM] * 5,
        out_shape=[near(shape)] * 4 + [half(TOKEN)],
        compiler_params=limit(VMEM_LIMIT),
        name="next_block",
    )(block, *map(in_near, (occ, virt, virt_back)), hold)


def inner_kernel(count, *refs):
    out, token = refs[2 * count :]
    token[...] = jnp.zeros_like(token)
    out[...] = long_dot(refs[:count], refs[count : 2 * count], out.shape[1] - out.shape[0]).astype(jnp.bfloat16)


def inner_chi(lefts, rights):
    rows = sum(left.shape[0] for left in lefts)
    wide = rows + lefts[-1].shape[0]
    return pl.pallas_call(
        functools.partial(inner_kernel, len(lefts)),
        in_specs=[VMEM] * (2 * len(lefts)),
        out_specs=[VMEM, VMEM],
        out_shape=[near((rows, wide)), half(TOKEN)],
        compiler_params=limit(VMEM_LIMIT),
        name="inner_chi",
    )(*map(in_near, lefts + rights))


def last_kernel(count, block, place, inner, *refs):
    right_backs, left_backs, out = refs[:count], refs[count : 2 * count], refs[2 * count]
    square = left_backs[0].shape[1]
    rows = block.shape[1]
    came = block.at[0, :, pl.ds(0, square)]
    aside = jnp.zeros((rows, inner.shape[1] - 2 * rows), jnp.float32)
    bottom = long_dot([came], right_backs, rows)
    bottom = bottom + jnp.concatenate([aside, block[0, :, square:].astype(jnp.float32)], 1)
    columns = long_dot(left_backs, [came], -rows)
    head, tail = inner[:, : -2 * rows], inner[:, -2 * rows :]
    top = jnp.concatenate([head, tail + columns.astype(jnp.bfloat16)], 1)
    total = jnp.concatenate([top, bottom.astype(jnp.bfloat16)], 0)
    out[...] = dot(place[...], total).astype(jnp.bfloat16)


def last_block(block, place, inner, right_backs, left_backs):
    return pl.pallas_call(
        functools.partial(last_kernel, len(left_backs)),
        in_specs=[VMEM] * (3 + 2 * len(left_backs)),
        out_specs=VMEM,
        out_shape=half(place.shape),
        compiler_params=limit(VMEM_LIMIT),
        name="last_block",
    )(block, *map(in_near, (place, inner, *right_backs, *left_backs)))


def finish_kernel(kcount, place, got, metric, chi, screen):
    rows, total = chi.shape
    blocks = 2 * kcount
    width = total // blocks
    placed = dot(place[...], got[...])
    low = iota((rows, LANES), 1) < width

    def block(t):
        straight, turned = None, None
        for j in range(kcount):
            at = (j * blocks + t) * rows
            piece = placed[at : at + rows, j // 2 * LANES : (j // 2 + 1) * LANES]
            if j % 2 == t % 2:
                straight = piece if straight is None else straight + piece
            else:
                turned = piece if turned is None else turned + piece
        return straight + pltpu.roll(turned, width, 1)

    for t in range(0, blocks, 2):
        chi[:, t * width : (t + 2) * width] = jnp.where(low, block(t), block(t + 1))
    screen[...] = dot(chi[...].astype(jnp.bfloat16), metric[...])


def finish(place, got, metric, kcount):
    total = metric.shape[0]
    rows = place.shape[0] // (2 * kcount * kcount)
    return pl.pallas_call(
        functools.partial(finish_kernel, kcount),
        in_specs=[VMEM] * 3,
        out_specs=[VMEM, VMEM],
        out_shape=[jax.ShapeDtypeStruct((rows, total), jnp.float32)] * 2,
        compiler_params=limit(VMEM_LIMIT),
        name="finish",
    )(place, got, metric)


def placing_kernel(hits, out):
    high, wide = hits.shape
    rows = out.shape[0] // high
    down = one(iota((high * rows, high), 0) // rows == iota((high * rows, high), 1))
    across = one(iota((wide * rows, wide), 0) // rows == iota((wide * rows, wide), 1))
    spread = dot_nt(dot(down, hits[...]).astype(jnp.bfloat16), across)
    same = iota(out.shape, 0) % rows == iota(out.shape, 1) % rows
    out[...] = jnp.where(same, spread, 0.0).astype(jnp.bfloat16)


def placing(hits, rows):
    return pl.pallas_call(
        placing_kernel,
        in_specs=[VMEM],
        out_specs=VMEM,
        out_shape=half((hits.shape[0] * rows, hits.shape[1] * rows)),
        compiler_params=limit(VMEM_LIMIT),
        name="placing",
    )(hits)


def swap(array, axes, step):
    count = lax.axis_size(axes)
    return lax.ppermute(array, axes, [(i, i ^ step) for i in range(count)])


def join_kernel(axis, step, own, other, *refs):
    out = refs[-1]
    upper = (lax.axis_index(axis) & step) != 0
    out[0] = jnp.where(upper, other[...], own[...])
    out[1] = jnp.where(upper, own[...], other[...])


def gathered(array, axis, step, hold=None):
    other = swap(array, axis, step)
    return pl.pallas_call(
        functools.partial(join_kernel, axis, step),
        in_specs=[VMEM] * (2 + (hold is not None)),
        out_specs=VMEM,
        out_shape=half((2,) + array.shape),
        compiler_params=limit(SMALL_LIMIT),
        name="join",
    )(array, other, *([] if hold is None else [hold]))


def gather_metric(out, total, own_rows, pairs, kcount, hold):
    ri_count, pair_count = lax.axis_size("ri"), lax.axis_size("pair")
    chips = ri_count // 4
    _, rows, wide = out.shape
    step = 4
    while step < ri_count:
        out = gathered(out, "ri", step).reshape(-1, rows, wide)
        step *= 2
    step = 1
    while step < pair_count:
        out = gathered(out, "pair", step, hold if step == 1 else None).reshape(-1, rows, wide)
        step *= 2
    all_ids = out.reshape(pair_count, chips, rows, wide)[:, 0, :pairs, total : total + kcount]
    out = out[:, :, :total].reshape(-1, rows // 2, total)[:, :own_rows]
    out = gathered(out, "ri", 1).swapaxes(0, 1).reshape(-1, total)
    return out, all_ids.reshape(-1, kcount)


def shards(three_c, green_occ, green_virt, pair_size, ri_ids, coulomb):
    everyone = ("pair", "ri")
    ri_count = lax.axis_size("ri")
    devices = lax.axis_size(everyone)
    kcount = ri_ids.shape[1]
    blocks = 2 * kcount
    pairs, _, rows, square = three_c.shape
    out_rows, total = coulomb.shape
    three_c = three_c.reshape(pairs, rows, square)
    slots = jnp.arange(kcount, dtype=jnp.int32)
    block_ids = jnp.arange(blocks, dtype=jnp.int32)
    riding_rows = max(16, out_rows)
    riding = jnp.pad(coulomb, ((0, riding_rows - out_rows), (0, 0)))

    parts, token = {}, None
    last = ri_count - 1
    for step in [2, 1] + list(range(3, last)):
        part, token = pick(three_c, step, coulomb=riding if step == 2 else None, hold=token)
        parts[step] = swap(part, "ri", step)
    part, token = corner(three_c, last, green_occ, green_virt, pair_size, token)
    parts[last] = swap(part, "ri", last)
    occ, virt, virt_back, place, left, right, left_back, right_back, token = first_blocks(
        three_c, parts[1], green_occ, green_virt, pair_size, ri_ids, token
    )
    lefts, rights, left_backs, right_backs = [left], [right], [left_back], [right_back]
    first_token = token
    for step in range(2, last):
        left, right, left_back, right_back, token = next_block(parts[step], occ, virt, virt_back, token, square)
        lefts.append(left)
        rights.append(right)
        left_backs.append(left_back)
        right_backs.append(right_back)
    inner, token = inner_chi(lefts, rights)
    pieces = last_block(parts[last], place, inner, right_backs, left_backs)

    slot = jnp.arange(pairs, dtype=jnp.int32)[:, None] ^ slots[None, :]
    relative = jnp.sum(jnp.where(slot[:, :, None] == slots, ri_ids[:, None, :], 0), 2)
    ids = jnp.pad(relative.astype(jnp.bfloat16), ((0, 2 * riding_rows - pairs), (0, LANES - kcount)))
    metric = rows_along_x(parts[2], riding, ids, first_token)
    metric, all_ids = gather_metric(metric, total, out_rows, pairs, kcount, token)
    hits = all_ids.T[:, None, :] == block_ids.astype(jnp.bfloat16)[None, :, None]
    placed = placing(hits.astype(jnp.bfloat16).reshape(kcount * blocks, devices), out_rows)

    got = lax.all_to_all(pieces.reshape(devices, out_rows, kcount * rows), everyone, 0, 0, tiled=True)
    return tuple(finish(placed, got.reshape(devices * out_rows, kcount * rows), metric, kcount))


def solution(mesh):
    placed = (
        P(("snap", "pair"), "ri", None, None),
        P(("snap", "pair"), None, None),
        P(("snap", "pair"), None, None),
        P(("snap", "pair")),
        P(("snap", "pair"), None),
        P(("snap", "pair", "ri"), None),
    )
    return jax.shard_map(
        shards,
        mesh=mesh,
        in_specs=placed,
        out_specs=(P(("snap", "pair", "ri"), None), P(("snap", "pair", "ri"), None)),
        check_vma=False,
    )
```

```python
import functools

import jax
import jax.numpy as jnp
from jax import lax
from jax.experimental import pallas as pl
from jax.experimental.pallas import tpu as pltpu
from jax.sharding import PartitionSpec as P

LANES = 128
SUB = 8
TOKEN = (16, 128)
VMEM_LIMIT = 20 * 1024 * 1024
SMALL_LIMIT = 4 * 1024 * 1024
VMEM = pl.BlockSpec(memory_space=pltpu.VMEM)
SMEM = pl.BlockSpec(memory_space=pltpu.SMEM)
ANY = pl.BlockSpec(memory_space=pl.ANY)


def iota(shape, dim):
    return lax.broadcasted_iota(jnp.int32, shape, dim)


def one(hit):
    return jnp.where(hit, 1.0, 0.0).astype(jnp.bfloat16)


def dot(a, b):
    return jnp.dot(a, b, preferred_element_type=jnp.float32)


def dot_nt(a, b):
    return lax.dot_general(a, b, (((1,), (1,)), ((), ())), preferred_element_type=jnp.float32)


def half(shape):
    return jax.ShapeDtypeStruct(shape, jnp.bfloat16)


def far(shape):
    return pltpu.HBM(shape, jnp.bfloat16)


def near(shape):
    return pltpu.VMEM(shape, jnp.bfloat16)


def in_near(array):
    return pltpu.with_memory_space_constraint(array, pltpu.VMEM)


def in_far(array):
    return pltpu.with_memory_space_constraint(array, pltpu.HBM)


def started(sems, pairs):
    copies = [pltpu.make_async_copy(a, b, sems.at[i]) for i, (a, b) in enumerate(pairs)]
    for copy in copies:
        copy.start()
    return copies


def finished(copies):
    for copy in copies:
        copy.wait()


def limit(size):
    return pltpu.CompilerParams(vmem_limit_bytes=size)


def pick_kernel(step, riding, *refs):
    three_c = refs[0]
    out, token, sems = refs[-3:]
    token[...] = jnp.zeros_like(token)
    _, count, _ = out.shape
    square = three_c.shape[2]
    pairs = [(three_c.at[lax.axis_index("ri") ^ step], out.at[0, :, pl.ds(0, square)])]
    if riding:
        coulomb = refs[1]
        rows, total = coulomb.shape
        fold = count // rows
        wide = total // fold
        for i in range(fold):
            there = out.at[0, pl.ds(i * rows, rows), pl.ds(square, wide)]
            pairs.append((coulomb.at[:, pl.ds(i * wide, wide)], there))
    finished(started(sems, pairs))


def pick(three_c, step, coulomb=None, hold=None):
    _, count, square = three_c.shape
    riding = coulomb is not None
    operands = [in_far(three_c)] + [in_far(a) for a in (coulomb,) if riding] + [a for a in (hold,) if a is not None]
    extra = coulomb.size // count if riding else 0
    rides = count // coulomb.shape[0] if riding else 0
    return pl.pallas_call(
        functools.partial(pick_kernel, step, riding),
        in_specs=[ANY] * (1 + riding) + [VMEM] * (hold is not None),
        out_specs=[VMEM, VMEM],
        out_shape=[near((1, count, square + extra)), half(TOKEN)],
        scratch_shapes=[pltpu.SemaphoreType.DMA((1 + rides,))],
        compiler_params=limit(SMALL_LIMIT),
        name="pick",
    )(*operands)


def along_x_kernel(block, coulomb, ids, hold, out):
    rows, total = coulomb.shape
    upper = (lax.axis_index("ri") & 2) != 0
    own = coulomb[...]
    fold = block.shape[1] // rows
    tail = block[0, :, block.shape[2] - total // fold :]
    other = jnp.concatenate([tail[i * rows : (i + 1) * rows] for i in range(fold)], 1)
    out[0, :rows, :total] = jnp.where(upper, other, own)
    out[0, rows:, :total] = jnp.where(upper, own, other)
    out[0, :, total:] = ids[...]


def rows_along_x(block, coulomb, ids, hold):
    rows, total = coulomb.shape
    return pl.pallas_call(
        along_x_kernel,
        in_specs=[VMEM] * 4,
        out_specs=VMEM,
        out_shape=half((1, 2 * rows, total + LANES)),
        compiler_params=limit(SMALL_LIMIT),
        name="rows_along_x",
    )(block, coulomb, ids, hold)


def prepared(size, occ, virt, occ_out, virt_out, back_out=None):
    width = occ.shape[0]
    full = occ_out.shape[0]
    spread = one(iota((full, width), 0) % width == iota((full, width), 1))
    tiled = dot_nt(dot(spread, occ).astype(jnp.bfloat16), spread)
    same = iota((full, full), 0) // width == iota((full, full), 1) // width
    occ_out[...] = jnp.where(same, tiled, 0.0).astype(jnp.bfloat16)

    keep = (iota((width, width), 0) < size) & (iota((width, width), 1) < size)
    kept = jnp.where(keep, virt.astype(jnp.float32), 0.0).astype(jnp.bfloat16)
    side = virt_out.shape[0] // 2
    same = iota((side, 2 * side), 0) % SUB == iota((side, 2 * side), 1) % SUB
    for parity in range(2):
        wanted = 2 * (iota((side, width), 0) // SUB) + parity
        picked_rows = one(wanted == iota((side, width), 1))
        column = iota((2 * side, width), 0)
        wanted = 2 * (column % side // SUB) + (column // side + parity) % 2
        picked_columns = one(wanted == iota((2 * side, width), 1))
        for target, product in ((virt_out, dot), (back_out, dot_nt)):
            if target is not None:
                part = dot_nt(product(picked_rows, kept).astype(jnp.bfloat16), picked_columns)
                target[parity * side : (parity + 1) * side, :] = jnp.where(same, part, 0.0).astype(jnp.bfloat16)


def times_occ(block, occ, left, product=dot):
    rows, square = left.shape
    full = occ.shape[0]
    wide = [block[:, c * full : (c + 1) * full] for c in range(square // full)]
    out = product(jnp.concatenate(wide, 0), occ[...]).astype(jnp.bfloat16)
    for c in range(square // full):
        left[:, c * full : (c + 1) * full] = out[c * rows : (c + 1) * rows]


def times_virt(virt, block, right):
    rows, square = right.shape
    chunks = square // LANES
    side = chunks * SUB
    low = iota((side, 2 * LANES), 1) % LANES < LANES // 2
    for row in range(0, rows, 2 * SUB):
        tile = block[row : row + 2 * SUB, :square].astype(jnp.float32)
        plain, turned = [], []
        for i in range(2):
            part = tile[i * SUB : (i + 1) * SUB]
            stacked = jnp.concatenate([part[:, c * LANES : (c + 1) * LANES] for c in range(chunks)], 0)
            plain.append(stacked)
            turned.append(pltpu.roll(stacked, LANES // 2, 1))
        operand = jnp.concatenate([jnp.concatenate(plain, 1), jnp.concatenate(turned, 1)], 0)
        out = dot(virt[...], operand.astype(jnp.bfloat16))
        out = jnp.where(low, out[:side], out[side:])
        for c in range(chunks):
            piece = out[c * SUB : (c + 1) * SUB]
            piece = jnp.concatenate([piece[:, :LANES], piece[:, LANES:]], 0)
            right[row : row + 2 * SUB, c * LANES : (c + 1) * LANES] = piece.astype(jnp.bfloat16)


def long_dot(lefts, rights, pad=0):
    square = lefts[0].shape[1]
    step = 1024
    total = None
    for c in range(0, square, step):
        a = jnp.concatenate([ref[:, c : c + step] for ref in lefts], 0)
        b = [ref[:, c : c + step] for ref in rights]
        zeros = [jnp.zeros((abs(pad), step), jnp.bfloat16)] if pad else []
        b = jnp.concatenate(b + zeros if pad > 0 else zeros + b, 0)
        part = dot_nt(a, b)
        total = part if total is None else total + part
    return total


def corner_kernel(step, sizes, three_c, occ, virt, hold, out, token, occ_wide, virt_wide, left, right, sem):
    token[...] = jnp.zeros_like(token)
    there = lax.axis_index("ri") ^ step
    rows, square = left.shape
    block = out.at[0, :, pl.ds(0, square)]
    copy = pltpu.make_async_copy(three_c.at[there], block, sem)
    copy.start()
    prepared(sizes[there], occ[there], virt[there], occ_wide, virt_wide)
    copy.wait()
    times_occ(block, occ_wide, left)
    times_virt(virt_wide, block, right)
    out[0, :, square:] = long_dot([left], [right], -rows).astype(jnp.bfloat16)


def corner(three_c, step, occ, virt, sizes, hold):
    _, rows, square = three_c.shape
    width = occ.shape[-1]
    shapes = [(4 * width, 4 * width), (SUB * width, SUB * width), (rows, square), (rows, square)]
    return pl.pallas_call(
        functools.partial(corner_kernel, step),
        in_specs=[SMEM, ANY, VMEM, VMEM, VMEM],
        out_specs=[VMEM, VMEM],
        out_shape=[near((1, rows, square + 2 * rows)), half(TOKEN)],
        scratch_shapes=[pltpu.VMEM(shape, jnp.bfloat16) for shape in shapes] + [pltpu.SemaphoreType.DMA],
        compiler_params=limit(VMEM_LIMIT),
        name="corner",
    )(sizes, in_far(three_c), occ, virt, hold)


def first_kernel(sizes, ids, three_c, other, occ, virt, hold, *refs):
    occ_out, virt_out, back_out, place, left, right, left_back, right_back, token, own, sem = refs
    token[...] = jnp.zeros_like(token)
    here = lax.axis_index("ri")
    copy = pltpu.make_async_copy(three_c.at[here], own, sem)
    copy.start()
    prepared(sizes[here], occ[here], virt[here], occ_out, virt_out, back_out)
    rows, square = own.shape
    column = iota(place.shape, 1)
    wanted = jnp.zeros(place.shape, jnp.int32)
    for j in range(ids.shape[1]):
        wanted = jnp.where(column // rows == j, ids[here, here ^ j], wanted)
    row = iota(place.shape, 0)
    place[...] = one((row // rows == wanted) & (row % rows == column % rows))
    copy.wait()
    for i, block in enumerate((own, other.at[0])):
        at = slice(i * rows, (i + 1) * rows)
        times_occ(block, occ_out, left.at[at])
        times_virt(virt_out, block, right.at[at])
        times_virt(back_out, left.at[at], left_back.at[at])
        times_occ(right.at[at], occ_out, right_back.at[at], dot_nt)


def first_blocks(three_c, other, occ, virt, sizes, ids, hold):
    _, rows, square = three_c.shape
    width = occ.shape[-1]
    kcount = ids.shape[1]
    shapes = [(4 * width, 4 * width)] + [(SUB * width, SUB * width)] * 2
    shapes += [(2 * kcount * rows, kcount * rows)] + [(2 * rows, square)] * 4
    return pl.pallas_call(
        first_kernel,
        in_specs=[SMEM, SMEM, ANY] + [VMEM] * 4,
        out_specs=[VMEM] * 9,
        out_shape=[near(shape) for shape in shapes] + [half(TOKEN)],
        scratch_shapes=[pltpu.VMEM((rows, square), jnp.bfloat16), pltpu.SemaphoreType.DMA],
        compiler_params=limit(VMEM_LIMIT),
        name="first_blocks",
    )(sizes, ids, in_far(three_c), other, occ, virt, hold)


def next_kernel(block, occ, virt, virt_back, hold, left, right, left_back, right_back, token):
    token[...] = jnp.zeros_like(token)
    times_occ(block.at[0], occ, left)
    times_virt(virt, block.at[0], right)
    times_virt(virt_back, left, left_back)
    times_occ(right, occ, right_back, dot_nt)


def next_block(block, occ, virt, virt_back, hold, square):
    shape = (block.shape[1], square)
    return pl.pallas_call(
        next_kernel,
        in_specs=[VMEM] * 5,
        out_specs=[VMEM] * 5,
        out_shape=[near(shape)] * 4 + [half(TOKEN)],
        compiler_params=limit(VMEM_LIMIT),
        name="next_block",
    )(block, *map(in_near, (occ, virt, virt_back)), hold)


def inner_kernel(count, *refs):
    out, token = refs[2 * count :]
    token[...] = jnp.zeros_like(token)
    out[...] = long_dot(refs[:count], refs[count : 2 * count], out.shape[1] - out.shape[0]).astype(jnp.bfloat16)


def inner_chi(lefts, rights):
    rows = sum(left.shape[0] for left in lefts)
    wide = rows + lefts[-1].shape[0]
    return pl.pallas_call(
        functools.partial(inner_kernel, len(lefts)),
        in_specs=[VMEM] * (2 * len(lefts)),
        out_specs=[VMEM, VMEM],
        out_shape=[near((rows, wide)), half(TOKEN)],
        compiler_params=limit(VMEM_LIMIT),
        name="inner_chi",
    )(*map(in_near, lefts + rights))


def last_kernel(count, block, place, inner, *refs):
    right_backs, left_backs, out = refs[:count], refs[count : 2 * count], refs[2 * count]
    square = left_backs[0].shape[1]
    rows = block.shape[1]
    came = block.at[0, :, pl.ds(0, square)]
    aside = jnp.zeros((rows, inner.shape[1] - 2 * rows), jnp.float32)
    bottom = long_dot([came], right_backs, rows)
    bottom = bottom + jnp.concatenate([aside, block[0, :, square:].astype(jnp.float32)], 1)
    columns = long_dot(left_backs, [came], -rows)
    head, tail = inner[:, : -2 * rows], inner[:, -2 * rows :]
    top = jnp.concatenate([head, tail + columns.astype(jnp.bfloat16)], 1)
    total = jnp.concatenate([top, bottom.astype(jnp.bfloat16)], 0)
    out[...] = dot(place[...], total).astype(jnp.bfloat16)


def last_block(block, place, inner, right_backs, left_backs):
    return pl.pallas_call(
        functools.partial(last_kernel, len(left_backs)),
        in_specs=[VMEM] * (3 + 2 * len(left_backs)),
        out_specs=VMEM,
        out_shape=half(place.shape),
        compiler_params=limit(VMEM_LIMIT),
        name="last_block",
    )(block, *map(in_near, (place, inner, *right_backs, *left_backs)))


def finish_kernel(kcount, place, got, metric, chi_out, screen_out, chi, screen, sems):
    rows, total = chi.shape
    blocks = 2 * kcount
    width = total // blocks
    group = place.shape[0] // (kcount * blocks)
    devices = got.shape[0] // rows
    low = iota((group, LANES), 1) < width
    for first in range(0, rows, group):
        part = got[...]
        if group < rows:
            part = jnp.concatenate([part[d * rows + first : d * rows + first + group] for d in range(devices)], 0)
        placed = dot(place[...], part)

        def block(t):
            straight, turned = None, None
            for j in range(kcount):
                at = (j * blocks + t) * group
                piece = placed[at : at + group, j // 2 * LANES : (j // 2 + 1) * LANES]
                if j % 2 == t % 2:
                    straight = piece if straight is None else straight + piece
                else:
                    turned = piece if turned is None else turned + piece
            return straight + pltpu.roll(turned, width, 1)

        for t in range(0, blocks, 2):
            chi[first : first + group, t * width : (t + 2) * width] = jnp.where(low, block(t), block(t + 1))
    copies = started(sems, [(chi, chi_out)])
    screen[...] = dot(chi[...].astype(jnp.bfloat16), metric[...])
    copies.append(pltpu.make_async_copy(screen, screen_out, sems.at[1]))
    copies[-1].start()
    finished(copies)


def finish(place, got, metric, kcount, rows):
    shape = (rows, metric.shape[0])
    return pl.pallas_call(
        functools.partial(finish_kernel, kcount),
        in_specs=[VMEM] * 3,
        out_specs=[ANY, ANY],
        out_shape=[jax.ShapeDtypeStruct(shape, jnp.float32)] * 2,
        scratch_shapes=[pltpu.VMEM(shape, jnp.float32)] * 2 + [pltpu.SemaphoreType.DMA((2,))],
        compiler_params=limit(VMEM_LIMIT),
        name="finish",
    )(place, got, metric)


def placing_kernel(hits, out):
    high, wide = hits.shape
    rows = out.shape[0] // high
    down = one(iota((high * rows, high), 0) // rows == iota((high * rows, high), 1))
    across = one(iota((wide * rows, wide), 0) // rows == iota((wide * rows, wide), 1))
    spread = dot_nt(dot(down, hits[...]).astype(jnp.bfloat16), across)
    same = iota(out.shape, 0) % rows == iota(out.shape, 1) % rows
    out[...] = jnp.where(same, spread, 0.0).astype(jnp.bfloat16)


def placing(hits, rows):
    return pl.pallas_call(
        placing_kernel,
        in_specs=[VMEM],
        out_specs=VMEM,
        out_shape=half((hits.shape[0] * rows, hits.shape[1] * rows)),
        compiler_params=limit(VMEM_LIMIT),
        name="placing",
    )(hits)


def swap(array, axes, step):
    count = lax.axis_size(axes)
    return lax.ppermute(array, axes, [(i, i ^ step) for i in range(count)])


def join_kernel(axis, step, own, other, *refs):
    out = refs[-1]
    upper = (lax.axis_index(axis) & step) != 0
    out[0] = jnp.where(upper, other[...], own[...])
    out[1] = jnp.where(upper, own[...], other[...])


def gathered(array, axis, step, hold=None):
    other = swap(array, axis, step)
    return pl.pallas_call(
        functools.partial(join_kernel, axis, step),
        in_specs=[VMEM] * (2 + (hold is not None)),
        out_specs=VMEM,
        out_shape=half((2,) + array.shape),
        compiler_params=limit(SMALL_LIMIT),
        name="join",
    )(array, other, *([] if hold is None else [hold]))


def gather_metric(out, total, own_rows, pairs, kcount, hold):
    ri_count, pair_count = lax.axis_size("ri"), lax.axis_size("pair")
    chips = ri_count // 4
    _, rows, wide = out.shape
    step = 4
    while step < ri_count:
        out = gathered(out, "ri", step).reshape(-1, rows, wide)
        step *= 2
    step = 1
    while step < pair_count:
        out = gathered(out, "pair", step, hold if step == 1 else None).reshape(-1, rows, wide)
        step *= 2
    all_ids = out.reshape(pair_count, chips, rows, wide)[:, 0, :pairs, total : total + kcount]
    out = out[:, :, :total].reshape(-1, rows // 2, total)[:, :own_rows]
    out = gathered(out, "ri", 1).swapaxes(0, 1).reshape(-1, total)
    return out, all_ids.reshape(-1, kcount)


def shards(three_c, green_occ, green_virt, pair_size, ri_ids, coulomb):
    everyone = ("pair", "ri")
    ri_count = lax.axis_size("ri")
    devices = lax.axis_size(everyone)
    kcount = ri_ids.shape[1]
    blocks = 2 * kcount
    pairs, _, rows, square = three_c.shape
    out_rows, total = coulomb.shape
    three_c = three_c.reshape(pairs, rows, square)
    slots = jnp.arange(kcount, dtype=jnp.int32)
    block_ids = jnp.arange(blocks, dtype=jnp.int32)
    riding_rows = max(16, out_rows)
    riding = jnp.pad(coulomb, ((0, riding_rows - out_rows), (0, 0)))

    parts, token = {}, None
    last = ri_count - 1
    for step in [2, 1] + list(range(3, last)):
        part, token = pick(three_c, step, coulomb=riding if step == 2 else None, hold=token)
        parts[step] = swap(part, "ri", step)
    part, token = corner(three_c, last, green_occ, green_virt, pair_size, token)
    parts[last] = swap(part, "ri", last)
    occ, virt, virt_back, place, left, right, left_back, right_back, token = first_blocks(
        three_c, parts[1], green_occ, green_virt, pair_size, ri_ids, token
    )
    lefts, rights, left_backs, right_backs = [left], [right], [left_back], [right_back]
    first_token = token
    for step in range(2, last):
        left, right, left_back, right_back, token = next_block(parts[step], occ, virt, virt_back, token, square)
        lefts.append(left)
        rights.append(right)
        left_backs.append(left_back)
        right_backs.append(right_back)
    inner, token = inner_chi(lefts, rights)
    pieces = last_block(parts[last], place, inner, right_backs, left_backs)

    slot = jnp.arange(pairs, dtype=jnp.int32)[:, None] ^ slots[None, :]
    relative = jnp.sum(jnp.where(slot[:, :, None] == slots, ri_ids[:, None, :], 0), 2)
    ids = jnp.pad(relative.astype(jnp.bfloat16), ((0, 2 * riding_rows - pairs), (0, LANES - kcount)))
    metric = rows_along_x(parts[2], riding, ids, first_token)
    metric, all_ids = gather_metric(metric, total, out_rows, pairs, kcount, token)
    hits = all_ids.T[:, None, :] == block_ids.astype(jnp.bfloat16)[None, :, None]
    placed = placing(hits.astype(jnp.bfloat16).reshape(kcount * blocks, devices), min(out_rows, 16))

    got = lax.all_to_all(pieces.reshape(devices, out_rows, kcount * rows), everyone, 0, 0, tiled=True)
    return tuple(finish(placed, got.reshape(devices * out_rows, kcount * rows), metric, kcount, out_rows))


def solution(mesh):
    placed = (
        P(("snap", "pair"), "ri", None, None),
        P(("snap", "pair"), None, None),
        P(("snap", "pair"), None, None),
        P(("snap", "pair")),
        P(("snap", "pair"), None),
        P(("snap", "pair", "ri"), None),
    )
    return jax.shard_map(
        shards,
        mesh=mesh,
        in_specs=placed,
        out_specs=(P(("snap", "pair", "ri"), None), P(("snap", "pair", "ri"), None)),
        check_vma=False,
    )
```

```python
import functools

import jax
import jax.numpy as jnp
from jax import lax
from jax.experimental import pallas as pl
from jax.experimental.pallas import tpu as pltpu
from jax.sharding import PartitionSpec as P

LANES = 128
SUB = 8
TOKEN = (16, 128)
VMEM_LIMIT = 20 * 1024 * 1024
SMALL_LIMIT = 4 * 1024 * 1024
VMEM = pl.BlockSpec(memory_space=pltpu.VMEM)
SMEM = pl.BlockSpec(memory_space=pltpu.SMEM)
ANY = pl.BlockSpec(memory_space=pl.ANY)


def iota(shape, dim):
    return lax.broadcasted_iota(jnp.int32, shape, dim)


def one(hit):
    return jnp.where(hit, 1.0, 0.0).astype(jnp.bfloat16)


def dot(a, b):
    return jnp.dot(a, b, preferred_element_type=jnp.float32)


def dot_nt(a, b):
    return lax.dot_general(a, b, (((1,), (1,)), ((), ())), preferred_element_type=jnp.float32)


def half(shape):
    return jax.ShapeDtypeStruct(shape, jnp.bfloat16)


def far(shape):
    return pltpu.HBM(shape, jnp.bfloat16)


def near(shape):
    return pltpu.VMEM(shape, jnp.bfloat16)


def in_near(array):
    return pltpu.with_memory_space_constraint(array, pltpu.VMEM)


def in_far(array):
    return pltpu.with_memory_space_constraint(array, pltpu.HBM)


def started(sems, pairs):
    copies = [pltpu.make_async_copy(a, b, sems.at[i]) for i, (a, b) in enumerate(pairs)]
    for copy in copies:
        copy.start()
    return copies


def finished(copies):
    for copy in copies:
        copy.wait()


def limit(size):
    return pltpu.CompilerParams(vmem_limit_bytes=size)


def pick_kernel(step, riding, *refs):
    three_c = refs[0]
    out, token, sems = refs[-3:]
    token[...] = jnp.zeros_like(token)
    _, count, _ = out.shape
    square = three_c.shape[2]
    pairs = [(three_c.at[lax.axis_index("ri") ^ step], out.at[0, :, pl.ds(0, square)])]
    if riding:
        coulomb = refs[1]
        rows, total = coulomb.shape
        fold = count // rows
        wide = total // fold
        for i in range(fold):
            there = out.at[0, pl.ds(i * rows, rows), pl.ds(square, wide)]
            pairs.append((coulomb.at[:, pl.ds(i * wide, wide)], there))
    finished(started(sems, pairs))


def pick(three_c, step, coulomb=None, hold=None):
    _, count, square = three_c.shape
    riding = coulomb is not None
    operands = [in_far(three_c)] + [in_far(a) for a in (coulomb,) if riding] + [a for a in (hold,) if a is not None]
    extra = coulomb.size // count if riding else 0
    rides = count // coulomb.shape[0] if riding else 0
    return pl.pallas_call(
        functools.partial(pick_kernel, step, riding),
        in_specs=[ANY] * (1 + riding) + [VMEM] * (hold is not None),
        out_specs=[VMEM, VMEM],
        out_shape=[near((1, count, square + extra)), half(TOKEN)],
        scratch_shapes=[pltpu.SemaphoreType.DMA((1 + rides,))],
        compiler_params=limit(SMALL_LIMIT),
        name="pick",
    )(*operands)


def along_x_kernel(block, coulomb, ids, hold, out):
    rows, total = coulomb.shape
    upper = (lax.axis_index("ri") & 2) != 0
    own = coulomb[...]
    fold = block.shape[1] // rows
    tail = block[0, :, block.shape[2] - total // fold :]
    other = jnp.concatenate([tail[i * rows : (i + 1) * rows] for i in range(fold)], 1)
    out[0, :rows, :total] = jnp.where(upper, other, own)
    out[0, rows:, :total] = jnp.where(upper, own, other)
    out[0, :, total:] = ids[...]


def rows_along_x(block, coulomb, ids, hold):
    rows, total = coulomb.shape
    return pl.pallas_call(
        along_x_kernel,
        in_specs=[VMEM] * 4,
        out_specs=VMEM,
        out_shape=half((1, 2 * rows, total + LANES)),
        compiler_params=limit(SMALL_LIMIT),
        name="rows_along_x",
    )(block, coulomb, ids, hold)


def prepared(size, occ, virt, occ_out, virt_out, back_out=None):
    width = occ.shape[0]
    full = occ_out.shape[0]
    spread = one(iota((full, width), 0) % width == iota((full, width), 1))
    tiled = dot_nt(dot(spread, occ).astype(jnp.bfloat16), spread)
    same = iota((full, full), 0) // width == iota((full, full), 1) // width
    occ_out[...] = jnp.where(same, tiled, 0.0).astype(jnp.bfloat16)

    keep = (iota((width, width), 0) < size) & (iota((width, width), 1) < size)
    kept = jnp.where(keep, virt.astype(jnp.float32), 0.0).astype(jnp.bfloat16)
    side = virt_out.shape[0] // 2
    same = iota((side, 2 * side), 0) % SUB == iota((side, 2 * side), 1) % SUB
    for parity in range(2):
        wanted = 2 * (iota((side, width), 0) // SUB) + parity
        picked_rows = one(wanted == iota((side, width), 1))
        column = iota((2 * side, width), 0)
        wanted = 2 * (column % side // SUB) + (column // side + parity) % 2
        picked_columns = one(wanted == iota((2 * side, width), 1))
        for target, product in ((virt_out, dot), (back_out, dot_nt)):
            if target is not None:
                part = dot_nt(product(picked_rows, kept).astype(jnp.bfloat16), picked_columns)
                target[parity * side : (parity + 1) * side, :] = jnp.where(same, part, 0.0).astype(jnp.bfloat16)


def times_occ(block, occ, left, product=dot):
    rows, square = left.shape
    full = occ.shape[0]
    wide = [block[:, c * full : (c + 1) * full] for c in range(square // full)]
    out = product(jnp.concatenate(wide, 0), occ[...]).astype(jnp.bfloat16)
    for c in range(square // full):
        left[:, c * full : (c + 1) * full] = out[c * rows : (c + 1) * rows]


def times_virt(virt, block, right):
    rows, square = right.shape
    chunks = square // LANES
    side = chunks * SUB
    low = iota((side, 2 * LANES), 1) % LANES < LANES // 2
    for row in range(0, rows, 2 * SUB):
        tile = block[row : row + 2 * SUB, :square].astype(jnp.float32)
        plain, turned = [], []
        for i in range(2):
            part = tile[i * SUB : (i + 1) * SUB]
            stacked = jnp.concatenate([part[:, c * LANES : (c + 1) * LANES] for c in range(chunks)], 0)
            plain.append(stacked)
            turned.append(pltpu.roll(stacked, LANES // 2, 1))
        operand = jnp.concatenate([jnp.concatenate(plain, 1), jnp.concatenate(turned, 1)], 0)
        out = dot(virt[...], operand.astype(jnp.bfloat16))
        out = jnp.where(low, out[:side], out[side:])
        for c in range(chunks):
            piece = out[c * SUB : (c + 1) * SUB]
            piece = jnp.concatenate([piece[:, :LANES], piece[:, LANES:]], 0)
            right[row : row + 2 * SUB, c * LANES : (c + 1) * LANES] = piece.astype(jnp.bfloat16)


def long_dot(lefts, rights, pad=0):
    square = lefts[0].shape[1]
    step = 1024
    total = None
    for c in range(0, square, step):
        a = jnp.concatenate([ref[:, c : c + step] for ref in lefts], 0)
        b = [ref[:, c : c + step] for ref in rights]
        zeros = [jnp.zeros((abs(pad), step), jnp.bfloat16)] if pad else []
        b = jnp.concatenate(b + zeros if pad > 0 else zeros + b, 0)
        part = dot_nt(a, b)
        total = part if total is None else total + part
    return total


def corner_kernel(step, sizes, three_c, occ, virt, hold, out, token, occ_wide, virt_wide, left, right, sem):
    token[...] = jnp.zeros_like(token)
    there = lax.axis_index("ri") ^ step
    rows, square = left.shape
    block = out.at[0, :, pl.ds(0, square)]
    copy = pltpu.make_async_copy(three_c.at[there], block, sem)
    copy.start()
    prepared(sizes[there], occ[there], virt[there], occ_wide, virt_wide)
    copy.wait()
    times_occ(block, occ_wide, left)
    times_virt(virt_wide, block, right)
    out[0, :, square:] = long_dot([left], [right], -rows).astype(jnp.bfloat16)


def corner(three_c, step, occ, virt, sizes, hold):
    _, rows, square = three_c.shape
    width = occ.shape[-1]
    shapes = [(4 * width, 4 * width), (SUB * width, SUB * width), (rows, square), (rows, square)]
    return pl.pallas_call(
        functools.partial(corner_kernel, step),
        in_specs=[SMEM, ANY, VMEM, VMEM, VMEM],
        out_specs=[VMEM, VMEM],
        out_shape=[near((1, rows, square + 2 * rows)), half(TOKEN)],
        scratch_shapes=[pltpu.VMEM(shape, jnp.bfloat16) for shape in shapes] + [pltpu.SemaphoreType.DMA],
        compiler_params=limit(VMEM_LIMIT),
        name="corner",
    )(sizes, in_far(three_c), occ, virt, hold)


def first_kernel(sizes, ids, three_c, other, occ, virt, hold, *refs):
    occ_out, virt_out, back_out, place, left, right, left_back, right_back, token, own, sem = refs
    token[...] = jnp.zeros_like(token)
    here = lax.axis_index("ri")
    copy = pltpu.make_async_copy(three_c.at[here], own, sem)
    copy.start()
    prepared(sizes[here], occ[here], virt[here], occ_out, virt_out, back_out)
    rows, square = own.shape
    column = iota(place.shape, 1)
    wanted = jnp.zeros(place.shape, jnp.int32)
    for j in range(ids.shape[1]):
        wanted = jnp.where(column // rows == j, ids[here, here ^ j], wanted)
    row = iota(place.shape, 0)
    place[...] = one((row // rows == wanted) & (row % rows == column % rows))
    copy.wait()
    for i, block in enumerate((own, other.at[0])):
        at = slice(i * rows, (i + 1) * rows)
        times_occ(block, occ_out, left.at[at])
        times_virt(virt_out, block, right.at[at])
        times_virt(back_out, left.at[at], left_back.at[at])
        times_occ(right.at[at], occ_out, right_back.at[at], dot_nt)


def first_blocks(three_c, other, occ, virt, sizes, ids, hold):
    _, rows, square = three_c.shape
    width = occ.shape[-1]
    kcount = ids.shape[1]
    shapes = [(4 * width, 4 * width)] + [(SUB * width, SUB * width)] * 2
    shapes += [(2 * kcount * rows, kcount * rows)] + [(2 * rows, square)] * 4
    return pl.pallas_call(
        first_kernel,
        in_specs=[SMEM, SMEM, ANY] + [VMEM] * 4,
        out_specs=[VMEM] * 9,
        out_shape=[near(shape) for shape in shapes] + [half(TOKEN)],
        scratch_shapes=[pltpu.VMEM((rows, square), jnp.bfloat16), pltpu.SemaphoreType.DMA],
        compiler_params=limit(VMEM_LIMIT),
        name="first_blocks",
    )(sizes, ids, in_far(three_c), other, occ, virt, hold)


def next_kernel(block, occ, virt, virt_back, hold, left, right, left_back, right_back, token):
    token[...] = jnp.zeros_like(token)
    times_occ(block.at[0], occ, left)
    times_virt(virt, block.at[0], right)
    times_virt(virt_back, left, left_back)
    times_occ(right, occ, right_back, dot_nt)


def next_block(block, occ, virt, virt_back, hold, square):
    shape = (block.shape[1], square)
    return pl.pallas_call(
        next_kernel,
        in_specs=[VMEM] * 5,
        out_specs=[VMEM] * 5,
        out_shape=[near(shape)] * 4 + [half(TOKEN)],
        compiler_params=limit(VMEM_LIMIT),
        name="next_block",
    )(block, *map(in_near, (occ, virt, virt_back)), hold)


def inner_kernel(count, *refs):
    out, token = refs[2 * count :]
    token[...] = jnp.zeros_like(token)
    out[...] = long_dot(refs[:count], refs[count : 2 * count], out.shape[1] - out.shape[0]).astype(jnp.bfloat16)


def inner_chi(lefts, rights):
    rows = sum(left.shape[0] for left in lefts)
    wide = rows + lefts[-1].shape[0]
    return pl.pallas_call(
        functools.partial(inner_kernel, len(lefts)),
        in_specs=[VMEM] * (2 * len(lefts)),
        out_specs=[VMEM, VMEM],
        out_shape=[near((rows, wide)), half(TOKEN)],
        compiler_params=limit(VMEM_LIMIT),
        name="inner_chi",
    )(*map(in_near, lefts + rights))


def last_kernel(count, block, place, inner, *refs):
    right_backs, left_backs, out = refs[:count], refs[count : 2 * count], refs[2 * count]
    square = left_backs[0].shape[1]
    rows = block.shape[1]
    came = block.at[0, :, pl.ds(0, square)]
    aside = jnp.zeros((rows, inner.shape[1] - 2 * rows), jnp.float32)
    bottom = long_dot([came], right_backs, rows)
    bottom = bottom + jnp.concatenate([aside, block[0, :, square:].astype(jnp.float32)], 1)
    columns = long_dot(left_backs, [came], -rows)
    head, tail = inner[:, : -2 * rows], inner[:, -2 * rows :]
    top = jnp.concatenate([head, tail + columns.astype(jnp.bfloat16)], 1)
    total = jnp.concatenate([top, bottom.astype(jnp.bfloat16)], 0)
    out[...] = dot(place[...], total).astype(jnp.bfloat16)


def last_block(block, place, inner, right_backs, left_backs):
    return pl.pallas_call(
        functools.partial(last_kernel, len(left_backs)),
        in_specs=[VMEM] * (3 + 2 * len(left_backs)),
        out_specs=VMEM,
        out_shape=half(place.shape),
        compiler_params=limit(VMEM_LIMIT),
        name="last_block",
    )(block, *map(in_near, (place, inner, *right_backs, *left_backs)))


def finish_kernel(kcount, place, got, metric, chi_out, screen_out, chi, screen, sems):
    rows, total = chi.shape
    blocks = 2 * kcount
    width = total // blocks
    group = place.shape[0] // (kcount * blocks)
    devices = got.shape[0] // rows
    low = iota((group, LANES), 1) < width
    for first in range(0, rows, group):
        part = got[...]
        if group < rows:
            part = jnp.concatenate([part[d * rows + first : d * rows + first + group] for d in range(devices)], 0)
        placed = dot(place[...], part)

        def block(t):
            straight, turned = None, None
            for j in range(kcount):
                at = (j * blocks + t) * group
                piece = placed[at : at + group, j // 2 * LANES : (j // 2 + 1) * LANES]
                if j % 2 == t % 2:
                    straight = piece if straight is None else straight + piece
                else:
                    turned = piece if turned is None else turned + piece
            return straight + pltpu.roll(turned, width, 1)

        for t in range(0, blocks, 2):
            chi[first : first + group, t * width : (t + 2) * width] = jnp.where(low, block(t), block(t + 1))
    copies = started(sems, [(chi, chi_out)])
    screen[...] = dot(chi[...].astype(jnp.bfloat16), metric[...])
    copies.append(pltpu.make_async_copy(screen, screen_out, sems.at[1]))
    copies[-1].start()
    finished(copies)


def finish(place, got, metric, kcount, rows):
    shape = (rows, metric.shape[0])
    return pl.pallas_call(
        functools.partial(finish_kernel, kcount),
        in_specs=[VMEM] * 3,
        out_specs=[ANY, ANY],
        out_shape=[jax.ShapeDtypeStruct(shape, jnp.float32)] * 2,
        scratch_shapes=[pltpu.VMEM(shape, jnp.float32)] * 2 + [pltpu.SemaphoreType.DMA((2,))],
        compiler_params=limit(VMEM_LIMIT),
        name="finish",
    )(place, got, metric)


def placing_kernel(hits, out):
    high, wide = hits.shape
    rows = out.shape[0] // high
    down = one(iota((high * rows, high), 0) // rows == iota((high * rows, high), 1))
    across = one(iota((wide * rows, wide), 0) // rows == iota((wide * rows, wide), 1))
    spread = dot_nt(dot(down, hits[...]).astype(jnp.bfloat16), across)
    same = iota(out.shape, 0) % rows == iota(out.shape, 1) % rows
    out[...] = jnp.where(same, spread, 0.0).astype(jnp.bfloat16)


def placing(hits, rows):
    return pl.pallas_call(
        placing_kernel,
        in_specs=[VMEM],
        out_specs=VMEM,
        out_shape=half((hits.shape[0] * rows, hits.shape[1] * rows)),
        compiler_params=limit(VMEM_LIMIT),
        name="placing",
    )(hits)


def swap(array, axes, step):
    count = lax.axis_size(axes)
    return lax.ppermute(array, axes, [(i, i ^ step) for i in range(count)])


def join_kernel(axis, step, own, other, *refs):
    out = refs[-1]
    upper = (lax.axis_index(axis) & step) != 0
    out[0] = jnp.where(upper, other[...], own[...])
    out[1] = jnp.where(upper, own[...], other[...])


def gathered(array, axis, step, hold=None):
    other = swap(array, axis, step)
    return pl.pallas_call(
        functools.partial(join_kernel, axis, step),
        in_specs=[VMEM] * (2 + (hold is not None)),
        out_specs=VMEM,
        out_shape=half((2,) + array.shape),
        compiler_params=limit(SMALL_LIMIT),
        name="join",
    )(array, other, *([] if hold is None else [hold]))


def gather_metric(out, total, own_rows, pairs, kcount, hold):
    ri_count, pair_count = lax.axis_size("ri"), lax.axis_size("pair")
    chips = ri_count // 4
    _, rows, wide = out.shape
    step = 4
    while step < ri_count:
        out = gathered(out, "ri", step).reshape(-1, rows, wide)
        step *= 2
    step = pair_count // 2
    bits = 0
    while step:
        out = gathered(out, "pair", step, None if bits else hold).reshape(-1, rows, wide)
        step //= 2
        bits += 1
    back = tuple(reversed(range(bits)))
    all_ids = out.reshape((2,) * bits + (chips, rows, wide))[..., 0, :pairs, total : total + kcount]
    all_ids = all_ids.transpose(back + (bits, bits + 1)).reshape(-1, kcount)
    out = out[:, :, :total].reshape(-1, rows // 2, total)[:, :own_rows]
    out = gathered(out, "ri", 1).reshape((2,) + (2,) * bits + (2 * chips, own_rows, total))
    out = out.transpose(tuple(1 + bit for bit in back) + (bits + 1, 0, bits + 2, bits + 3))
    return out.reshape(-1, total), all_ids


def shards(three_c, green_occ, green_virt, pair_size, ri_ids, coulomb):
    everyone = ("pair", "ri")
    ri_count = lax.axis_size("ri")
    devices = lax.axis_size(everyone)
    kcount = ri_ids.shape[1]
    blocks = 2 * kcount
    pairs, _, rows, square = three_c.shape
    out_rows, total = coulomb.shape
    three_c = three_c.reshape(pairs, rows, square)
    slots = jnp.arange(kcount, dtype=jnp.int32)
    block_ids = jnp.arange(blocks, dtype=jnp.int32)
    riding_rows = max(16, out_rows)
    riding = jnp.pad(coulomb, ((0, riding_rows - out_rows), (0, 0)))

    parts, token = {}, None
    last = ri_count - 1
    for step in [2, 1] + list(range(3, last)):
        part, token = pick(three_c, step, coulomb=riding if step == 2 else None, hold=token)
        parts[step] = swap(part, "ri", step)
    part, token = corner(three_c, last, green_occ, green_virt, pair_size, token)
    parts[last] = swap(part, "ri", last)
    occ, virt, virt_back, place, left, right, left_back, right_back, token = first_blocks(
        three_c, parts[1], green_occ, green_virt, pair_size, ri_ids, token
    )
    lefts, rights, left_backs, right_backs = [left], [right], [left_back], [right_back]
    first_token = token
    for step in range(2, last):
        left, right, left_back, right_back, token = next_block(parts[step], occ, virt, virt_back, token, square)
        lefts.append(left)
        rights.append(right)
        left_backs.append(left_back)
        right_backs.append(right_back)
    inner, token = inner_chi(lefts, rights)
    pieces = last_block(parts[last], place, inner, right_backs, left_backs)

    slot = jnp.arange(pairs, dtype=jnp.int32)[:, None] ^ slots[None, :]
    relative = jnp.sum(jnp.where(slot[:, :, None] == slots, ri_ids[:, None, :], 0), 2)
    ids = jnp.pad(relative.astype(jnp.bfloat16), ((0, 2 * riding_rows - pairs), (0, LANES - kcount)))
    metric = rows_along_x(parts[2], riding, ids, first_token)
    metric, all_ids = gather_metric(metric, total, out_rows, pairs, kcount, token)
    hits = all_ids.T[:, None, :] == block_ids.astype(jnp.bfloat16)[None, :, None]
    placed = placing(hits.astype(jnp.bfloat16).reshape(kcount * blocks, devices), min(out_rows, 16))

    got = lax.all_to_all(pieces.reshape(devices, out_rows, kcount * rows), everyone, 0, 0, tiled=True)
    return tuple(finish(placed, got.reshape(devices * out_rows, kcount * rows), metric, kcount, out_rows))


def solution(mesh):
    placed = (
        P(("snap", "pair"), "ri", None, None),
        P(("snap", "pair"), None, None),
        P(("snap", "pair"), None, None),
        P(("snap", "pair")),
        P(("snap", "pair"), None),
        P(("snap", "pair", "ri"), None),
    )
    return jax.shard_map(
        shards,
        mesh=mesh,
        in_specs=placed,
        out_specs=(P(("snap", "pair", "ri"), None), P(("snap", "pair", "ri"), None)),
        check_vma=False,
    )
```

```python
import functools

import jax
import jax.numpy as jnp
from jax import lax
from jax.experimental import pallas as pl
from jax.experimental.pallas import tpu as pltpu
from jax.sharding import PartitionSpec as P

LANES = 128
SUB = 8
TOKEN = (16, 128)
VMEM_LIMIT = 20 * 1024 * 1024
SMALL_LIMIT = 4 * 1024 * 1024
VMEM = pl.BlockSpec(memory_space=pltpu.VMEM)
SMEM = pl.BlockSpec(memory_space=pltpu.SMEM)
ANY = pl.BlockSpec(memory_space=pl.ANY)


def iota(shape, dim):
    return lax.broadcasted_iota(jnp.int32, shape, dim)


def one(hit):
    return jnp.where(hit, 1.0, 0.0).astype(jnp.bfloat16)


def dot(a, b):
    return jnp.dot(a, b, preferred_element_type=jnp.float32)


def dot_nt(a, b):
    return lax.dot_general(a, b, (((1,), (1,)), ((), ())), preferred_element_type=jnp.float32)


def half(shape):
    return jax.ShapeDtypeStruct(shape, jnp.bfloat16)


def far(shape):
    return pltpu.HBM(shape, jnp.bfloat16)


def near(shape):
    return pltpu.VMEM(shape, jnp.bfloat16)


def in_near(array):
    return pltpu.with_memory_space_constraint(array, pltpu.VMEM)


def in_far(array):
    return pltpu.with_memory_space_constraint(array, pltpu.HBM)


def started(sems, pairs):
    copies = [pltpu.make_async_copy(a, b, sems.at[i]) for i, (a, b) in enumerate(pairs)]
    for copy in copies:
        copy.start()
    return copies


def finished(copies):
    for copy in copies:
        copy.wait()


def limit(size):
    return pltpu.CompilerParams(vmem_limit_bytes=size)


def pick_kernel(step, riding, *refs):
    three_c = refs[0]
    out, token, sems = refs[-3:]
    token[...] = jnp.zeros_like(token)
    _, count, _ = out.shape
    square = three_c.shape[2]
    pairs = [(three_c.at[lax.axis_index("ri") ^ step], out.at[0, :, pl.ds(0, square)])]
    if riding:
        coulomb = refs[1]
        rows, total = coulomb.shape
        fold = count // rows
        wide = total // fold
        for i in range(fold):
            there = out.at[0, pl.ds(i * rows, rows), pl.ds(square, wide)]
            pairs.append((coulomb.at[:, pl.ds(i * wide, wide)], there))
    finished(started(sems, pairs))


def pick(three_c, step, coulomb=None, hold=None):
    _, count, square = three_c.shape
    riding = coulomb is not None
    operands = [in_far(three_c)] + [in_far(a) for a in (coulomb,) if riding] + [a for a in (hold,) if a is not None]
    extra = coulomb.size // count if riding else 0
    rides = count // coulomb.shape[0] if riding else 0
    return pl.pallas_call(
        functools.partial(pick_kernel, step, riding),
        in_specs=[ANY] * (1 + riding) + [VMEM] * (hold is not None),
        out_specs=[VMEM, VMEM],
        out_shape=[near((1, count, square + extra)), half(TOKEN)],
        scratch_shapes=[pltpu.SemaphoreType.DMA((1 + rides,))],
        compiler_params=limit(SMALL_LIMIT),
        name="pick",
    )(*operands)


def along_x_kernel(block, coulomb, ids, hold, out):
    rows, total = coulomb.shape
    upper = (lax.axis_index("ri") & 2) != 0
    own = coulomb[...]
    fold = block.shape[1] // rows
    tail = block[0, :, block.shape[2] - total // fold :]
    other = jnp.concatenate([tail[i * rows : (i + 1) * rows] for i in range(fold)], 1)
    out[0, :rows, :total] = jnp.where(upper, other, own)
    out[0, rows:, :total] = jnp.where(upper, own, other)
    out[0, :, total:] = ids[...]


def rows_along_x(block, coulomb, ids, hold):
    rows, total = coulomb.shape
    return pl.pallas_call(
        along_x_kernel,
        in_specs=[VMEM] * 4,
        out_specs=VMEM,
        out_shape=half((1, 2 * rows, total + LANES)),
        compiler_params=limit(SMALL_LIMIT),
        name="rows_along_x",
    )(block, coulomb, ids, hold)


def prepared(size, occ, virt, occ_out, virt_out, back_out=None):
    width = occ.shape[0]
    full = occ_out.shape[0]
    spread = one(iota((full, width), 0) % width == iota((full, width), 1))
    tiled = dot_nt(dot(spread, occ).astype(jnp.bfloat16), spread)
    same = iota((full, full), 0) // width == iota((full, full), 1) // width
    occ_out[...] = jnp.where(same, tiled, 0.0).astype(jnp.bfloat16)

    keep = (iota((width, width), 0) < size) & (iota((width, width), 1) < size)
    kept = jnp.where(keep, virt.astype(jnp.float32), 0.0).astype(jnp.bfloat16)
    side = virt_out.shape[0] // 2
    same = iota((side, 2 * side), 0) % SUB == iota((side, 2 * side), 1) % SUB
    for parity in range(2):
        wanted = 2 * (iota((side, width), 0) // SUB) + parity
        picked_rows = one(wanted == iota((side, width), 1))
        column = iota((2 * side, width), 0)
        wanted = 2 * (column % side // SUB) + (column // side + parity) % 2
        picked_columns = one(wanted == iota((2 * side, width), 1))
        for target, product in ((virt_out, dot), (back_out, dot_nt)):
            if target is not None:
                part = dot_nt(product(picked_rows, kept).astype(jnp.bfloat16), picked_columns)
                target[parity * side : (parity + 1) * side, :] = jnp.where(same, part, 0.0).astype(jnp.bfloat16)


def times_occ(block, occ, left, product=dot):
    rows, square = left.shape
    full = occ.shape[0]
    wide = [block[:, c * full : (c + 1) * full] for c in range(square // full)]
    out = product(jnp.concatenate(wide, 0), occ[...]).astype(jnp.bfloat16)
    for c in range(square // full):
        left[:, c * full : (c + 1) * full] = out[c * rows : (c + 1) * rows]


def times_virt(virt, block, right):
    rows, square = right.shape
    chunks = square // LANES
    side = chunks * SUB
    low = iota((side, 2 * LANES), 1) % LANES < LANES // 2
    for row in range(0, rows, 2 * SUB):
        tile = block[row : row + 2 * SUB, :square].astype(jnp.float32)
        plain, turned = [], []
        for i in range(2):
            part = tile[i * SUB : (i + 1) * SUB]
            stacked = jnp.concatenate([part[:, c * LANES : (c + 1) * LANES] for c in range(chunks)], 0)
            plain.append(stacked)
            turned.append(pltpu.roll(stacked, LANES // 2, 1))
        operand = jnp.concatenate([jnp.concatenate(plain, 1), jnp.concatenate(turned, 1)], 0)
        out = dot(virt[...], operand.astype(jnp.bfloat16))
        out = jnp.where(low, out[:side], out[side:])
        for c in range(chunks):
            piece = out[c * SUB : (c + 1) * SUB]
            piece = jnp.concatenate([piece[:, :LANES], piece[:, LANES:]], 0)
            right[row : row + 2 * SUB, c * LANES : (c + 1) * LANES] = piece.astype(jnp.bfloat16)


def long_dot(lefts, rights, pad=0):
    square = lefts[0].shape[1]
    step = 1024
    total = None
    for c in range(0, square, step):
        a = jnp.concatenate([ref[:, c : c + step] for ref in lefts], 0)
        b = [ref[:, c : c + step] for ref in rights]
        zeros = [jnp.zeros((abs(pad), step), jnp.bfloat16)] if pad else []
        b = jnp.concatenate(b + zeros if pad > 0 else zeros + b, 0)
        part = dot_nt(a, b)
        total = part if total is None else total + part
    return total


def corner_kernel(step, sizes, three_c, occ, virt, hold, out, token, occ_wide, virt_wide, left, right, sem):
    token[...] = jnp.zeros_like(token)
    there = lax.axis_index("ri") ^ step
    rows, square = left.shape
    block = out.at[0, :, pl.ds(0, square)]
    copy = pltpu.make_async_copy(three_c.at[there], block, sem)
    copy.start()
    prepared(sizes[there], occ[there], virt[there], occ_wide, virt_wide)
    copy.wait()
    times_occ(block, occ_wide, left)
    times_virt(virt_wide, block, right)
    out[0, :, square:] = long_dot([left], [right], -rows).astype(jnp.bfloat16)


def corner(three_c, step, occ, virt, sizes, hold):
    _, rows, square = three_c.shape
    width = occ.shape[-1]
    shapes = [(4 * width, 4 * width), (SUB * width, SUB * width), (rows, square), (rows, square)]
    return pl.pallas_call(
        functools.partial(corner_kernel, step),
        in_specs=[SMEM, ANY, VMEM, VMEM, VMEM],
        out_specs=[VMEM, VMEM],
        out_shape=[near((1, rows, square + 2 * rows)), half(TOKEN)],
        scratch_shapes=[pltpu.VMEM(shape, jnp.bfloat16) for shape in shapes] + [pltpu.SemaphoreType.DMA],
        compiler_params=limit(VMEM_LIMIT),
        name="corner",
    )(sizes, in_far(three_c), occ, virt, hold)


def first_kernel(sizes, ids, three_c, other, occ, virt, hold, *refs):
    occ_out, virt_out, back_out, place, left, right, left_back, right_back, token, own, sem = refs
    token[...] = jnp.zeros_like(token)
    here = lax.axis_index("ri")
    copy = pltpu.make_async_copy(three_c.at[here], own, sem)
    copy.start()
    prepared(sizes[here], occ[here], virt[here], occ_out, virt_out, back_out)
    rows, square = own.shape
    column = iota(place.shape, 1)
    wanted = jnp.zeros(place.shape, jnp.int32)
    for j in range(ids.shape[1]):
        wanted = jnp.where(column // rows == j, ids[here, here ^ j], wanted)
    row = iota(place.shape, 0)
    place[...] = one((row // rows == wanted) & (row % rows == column % rows))
    copy.wait()
    for i, block in enumerate((own, other.at[0])):
        at = slice(i * rows, (i + 1) * rows)
        times_occ(block, occ_out, left.at[at])
        times_virt(virt_out, block, right.at[at])
        times_virt(back_out, left.at[at], left_back.at[at])
        times_occ(right.at[at], occ_out, right_back.at[at], dot_nt)


def first_blocks(three_c, other, occ, virt, sizes, ids, hold):
    _, rows, square = three_c.shape
    width = occ.shape[-1]
    kcount = ids.shape[1]
    shapes = [(4 * width, 4 * width)] + [(SUB * width, SUB * width)] * 2
    shapes += [(2 * kcount * rows, kcount * rows)] + [(2 * rows, square)] * 4
    return pl.pallas_call(
        first_kernel,
        in_specs=[SMEM, SMEM, ANY] + [VMEM] * 4,
        out_specs=[VMEM] * 9,
        out_shape=[near(shape) for shape in shapes] + [half(TOKEN)],
        scratch_shapes=[pltpu.VMEM((rows, square), jnp.bfloat16), pltpu.SemaphoreType.DMA],
        compiler_params=limit(VMEM_LIMIT),
        name="first_blocks",
    )(sizes, ids, in_far(three_c), other, occ, virt, hold)


def next_kernel(block, occ, virt, virt_back, hold, left, right, left_back, right_back, token):
    token[...] = jnp.zeros_like(token)
    times_occ(block.at[0], occ, left)
    times_virt(virt, block.at[0], right)
    times_virt(virt_back, left, left_back)
    times_occ(right, occ, right_back, dot_nt)


def next_block(block, occ, virt, virt_back, hold, square):
    shape = (block.shape[1], square)
    return pl.pallas_call(
        next_kernel,
        in_specs=[VMEM] * 5,
        out_specs=[VMEM] * 5,
        out_shape=[near(shape)] * 4 + [half(TOKEN)],
        compiler_params=limit(VMEM_LIMIT),
        name="next_block",
    )(block, *map(in_near, (occ, virt, virt_back)), hold)


def inner_kernel(count, place, *refs):
    tail, head, token = refs[2 * count :]
    token[...] = jnp.zeros_like(token)
    high, wide = place.shape[1] - tail.shape[1] // 2, place.shape[1]
    inner = long_dot(refs[:count], refs[count : 2 * count], wide - high).astype(jnp.bfloat16)
    tail[...] = inner[:, head.shape[1] :]
    padded = jnp.concatenate([inner[:, : head.shape[1]], jnp.zeros((wide - high, head.shape[1]), jnp.bfloat16)], 0)
    head[...] = dot(place[...], padded).astype(jnp.bfloat16)


def inner_chi(place, lefts, rights):
    rows = sum(left.shape[0] for left in lefts)
    wide = rows + lefts[-1].shape[0]
    return pl.pallas_call(
        functools.partial(inner_kernel, len(lefts)),
        in_specs=[VMEM] * (1 + 2 * len(lefts)),
        out_specs=[VMEM] * 3,
        out_shape=[near((rows, LANES)), near((place.shape[0], wide - LANES)), half(TOKEN)],
        compiler_params=limit(VMEM_LIMIT),
        name="inner_chi",
    )(*map(in_near, [place] + lefts + rights))


def last_kernel(count, block, place, tail, head, *refs):
    right_backs, left_backs = refs[:count], refs[count : 2 * count]
    out = refs[2 * count]
    square = left_backs[0].shape[1]
    rows = block.shape[1]
    split = head.shape[1]
    came = block.at[0, :, pl.ds(0, square)]
    bottom = long_dot([came], right_backs, rows)
    early = jnp.concatenate([jnp.zeros((LANES - rows, split), jnp.bfloat16), bottom[:, :split].astype(jnp.bfloat16)], 0)
    low = bottom[:, split:] + block[0, :, square:].astype(jnp.float32)
    columns = long_dot(left_backs, [came], -rows)
    late = jnp.concatenate([tail[...] + columns.astype(jnp.bfloat16), low.astype(jnp.bfloat16)], 0)
    out[:, split:] = dot(place[...], late).astype(jnp.bfloat16)
    out[:, :split] = head[...] + dot(place[:, split:], early).astype(jnp.bfloat16)


def last_block(block, place, tail, head, right_backs, left_backs):
    return pl.pallas_call(
        functools.partial(last_kernel, len(left_backs)),
        in_specs=[VMEM] * (4 + 2 * len(left_backs)),
        out_specs=VMEM,
        out_shape=half(place.shape),
        compiler_params=limit(VMEM_LIMIT),
        name="last_block",
    )(block, *map(in_near, (place, tail, head, *right_backs, *left_backs)))


def finish_kernel(kcount, place, got, metric, chi_out, screen_out, chi, screen, sems):
    rows, total = chi.shape
    blocks = 2 * kcount
    width = total // blocks
    group = place.shape[0] // (kcount * blocks)
    devices = got.shape[0] // rows
    low = iota((group, LANES), 1) < width
    for first in range(0, rows, group):
        part = got[...]
        if group < rows:
            part = jnp.concatenate([part[d * rows + first : d * rows + first + group] for d in range(devices)], 0)
        step = 2 * blocks * group
        placed = [
            dot(place[h * step : (h + 1) * step, :], part[:, h * LANES : (h + 1) * LANES]) for h in range(kcount // 2)
        ]

        def block(t):
            straight, turned = None, None
            for j in range(kcount):
                at = (j % 2 * blocks + t) * group
                piece = placed[j // 2][at : at + group]
                if j % 2 == t % 2:
                    straight = piece if straight is None else straight + piece
                else:
                    turned = piece if turned is None else turned + piece
            return straight + pltpu.roll(turned, width, 1)

        for t in range(0, blocks, 2):
            chi[first : first + group, t * width : (t + 2) * width] = jnp.where(low, block(t), block(t + 1))
    copies = started(sems, [(chi, chi_out)])
    screen[...] = dot(chi[...].astype(jnp.bfloat16), metric[...])
    copies.append(pltpu.make_async_copy(screen, screen_out, sems.at[1]))
    copies[-1].start()
    finished(copies)


def finish(place, got, metric, kcount, rows):
    shape = (rows, metric.shape[0])
    return pl.pallas_call(
        functools.partial(finish_kernel, kcount),
        in_specs=[VMEM] * 3,
        out_specs=[ANY, ANY],
        out_shape=[jax.ShapeDtypeStruct(shape, jnp.float32)] * 2,
        scratch_shapes=[pltpu.VMEM(shape, jnp.float32)] * 2 + [pltpu.SemaphoreType.DMA((2,))],
        compiler_params=limit(VMEM_LIMIT),
        name="finish",
    )(place, got, metric)


def placing_kernel(hits, out):
    high, wide = hits.shape
    rows = out.shape[0] // high
    down = one(iota((high * rows, high), 0) // rows == iota((high * rows, high), 1))
    across = one(iota((wide * rows, wide), 0) // rows == iota((wide * rows, wide), 1))
    spread = dot_nt(dot(down, hits[...]).astype(jnp.bfloat16), across)
    same = iota(out.shape, 0) % rows == iota(out.shape, 1) % rows
    out[...] = jnp.where(same, spread, 0.0).astype(jnp.bfloat16)


def placing(hits, rows):
    return pl.pallas_call(
        placing_kernel,
        in_specs=[VMEM],
        out_specs=VMEM,
        out_shape=half((hits.shape[0] * rows, hits.shape[1] * rows)),
        compiler_params=limit(VMEM_LIMIT),
        name="placing",
    )(hits)


def swap(array, axes, step):
    count = lax.axis_size(axes)
    return lax.ppermute(array, axes, [(i, i ^ step) for i in range(count)])


def join_kernel(axis, step, own, other, *refs):
    out = refs[-1]
    upper = (lax.axis_index(axis) & step) != 0
    out[0] = jnp.where(upper, other[...], own[...])
    out[1] = jnp.where(upper, own[...], other[...])


def gathered(array, axis, step, hold=None):
    other = swap(array, axis, step)
    return pl.pallas_call(
        functools.partial(join_kernel, axis, step),
        in_specs=[VMEM] * (2 + (hold is not None)),
        out_specs=VMEM,
        out_shape=half((2,) + array.shape),
        compiler_params=limit(SMALL_LIMIT),
        name="join",
    )(array, other, *([] if hold is None else [hold]))


def gather_metric(out, total, own_rows, pairs, kcount, hold):
    ri_count, pair_count = lax.axis_size("ri"), lax.axis_size("pair")
    chips = ri_count // 4
    _, rows, wide = out.shape
    step = 4
    while step < ri_count:
        out = gathered(out, "ri", step).reshape(-1, rows, wide)
        step *= 2
    step = 1
    while step < pair_count:
        out = gathered(out, "pair", step, hold if step == 1 else None).reshape(-1, rows, wide)
        step *= 2
    all_ids = out.reshape(pair_count, chips, rows, wide)[:, 0, :pairs, total : total + kcount]
    out = out[:, :, :total].reshape(-1, rows // 2, total)[:, :own_rows]
    out = gathered(out, "ri", 1).swapaxes(0, 1).reshape(-1, total)
    return out, all_ids.reshape(-1, kcount)


def shards(three_c, green_occ, green_virt, pair_size, ri_ids, coulomb):
    everyone = ("pair", "ri")
    ri_count = lax.axis_size("ri")
    devices = lax.axis_size(everyone)
    kcount = ri_ids.shape[1]
    blocks = 2 * kcount
    pairs, _, rows, square = three_c.shape
    out_rows, total = coulomb.shape
    three_c = three_c.reshape(pairs, rows, square)
    slots = jnp.arange(kcount, dtype=jnp.int32)
    block_ids = jnp.arange(blocks, dtype=jnp.int32)
    riding_rows = max(16, out_rows)
    riding = jnp.pad(coulomb, ((0, riding_rows - out_rows), (0, 0)))

    parts, token = {}, None
    last = ri_count - 1
    for step in [2, 1] + list(range(3, last)):
        part, token = pick(three_c, step, coulomb=riding if step == 2 else None, hold=token)
        parts[step] = swap(part, "ri", step)
    part, token = corner(three_c, last, green_occ, green_virt, pair_size, token)
    parts[last] = swap(part, "ri", last)
    occ, virt, virt_back, place, left, right, left_back, right_back, token = first_blocks(
        three_c, parts[1], green_occ, green_virt, pair_size, ri_ids, token
    )
    lefts, rights, left_backs, right_backs = [left], [right], [left_back], [right_back]
    first_token = token
    for step in range(2, last):
        left, right, left_back, right_back, token = next_block(parts[step], occ, virt, virt_back, token, square)
        lefts.append(left)
        rights.append(right)
        left_backs.append(left_back)
        right_backs.append(right_back)
    tail, head, token = inner_chi(place, lefts, rights)
    pieces = last_block(parts[last], place, tail, head, right_backs, left_backs)

    slot = jnp.arange(pairs, dtype=jnp.int32)[:, None] ^ slots[None, :]
    relative = jnp.sum(jnp.where(slot[:, :, None] == slots, ri_ids[:, None, :], 0), 2)
    ids = jnp.pad(relative.astype(jnp.bfloat16), ((0, 2 * riding_rows - pairs), (0, LANES - kcount)))
    metric = rows_along_x(parts[2], riding, ids, first_token)
    metric, all_ids = gather_metric(metric, total, out_rows, pairs, kcount, token)
    hits = all_ids.T[:, None, :] == block_ids.astype(jnp.bfloat16)[None, :, None]
    placed = placing(hits.astype(jnp.bfloat16).reshape(kcount * blocks, devices), min(out_rows, 16))

    got = lax.all_to_all(pieces.reshape(devices, out_rows, kcount * rows), everyone, 0, 0, tiled=True)
    return tuple(finish(placed, got.reshape(devices * out_rows, kcount * rows), metric, kcount, out_rows))


def solution(mesh):
    placed = (
        P(("snap", "pair"), "ri", None, None),
        P(("snap", "pair"), None, None),
        P(("snap", "pair"), None, None),
        P(("snap", "pair")),
        P(("snap", "pair"), None),
        P(("snap", "pair", "ri"), None),
    )
    return jax.shard_map(
        shards,
        mesh=mesh,
        in_specs=placed,
        out_specs=(P(("snap", "pair", "ri"), None), P(("snap", "pair", "ri"), None)),
        check_vma=False,
    )
```

```python
import functools

import jax
import jax.numpy as jnp
from jax import lax
from jax.experimental import pallas as pl
from jax.experimental.pallas import tpu as pltpu
from jax.sharding import PartitionSpec as P

LANES = 128
SUB = 8
TOKEN = (16, 128)
VMEM_LIMIT = 20 * 1024 * 1024
SMALL_LIMIT = 4 * 1024 * 1024
VMEM = pl.BlockSpec(memory_space=pltpu.VMEM)
SMEM = pl.BlockSpec(memory_space=pltpu.SMEM)
ANY = pl.BlockSpec(memory_space=pl.ANY)


def iota(shape, dim):
    return lax.broadcasted_iota(jnp.int32, shape, dim)


def one(hit):
    return jnp.where(hit, 1.0, 0.0).astype(jnp.bfloat16)


def dot(a, b):
    return jnp.dot(a, b, preferred_element_type=jnp.float32)


def dot_nt(a, b):
    return lax.dot_general(a, b, (((1,), (1,)), ((), ())), preferred_element_type=jnp.float32)


def half(shape):
    return jax.ShapeDtypeStruct(shape, jnp.bfloat16)


def far(shape):
    return pltpu.HBM(shape, jnp.bfloat16)


def near(shape):
    return pltpu.VMEM(shape, jnp.bfloat16)


def in_near(array):
    return pltpu.with_memory_space_constraint(array, pltpu.VMEM)


def in_far(array):
    return pltpu.with_memory_space_constraint(array, pltpu.HBM)


def started(sems, pairs):
    copies = [pltpu.make_async_copy(a, b, sems.at[i]) for i, (a, b) in enumerate(pairs)]
    for copy in copies:
        copy.start()
    return copies


def finished(copies):
    for copy in copies:
        copy.wait()


def limit(size):
    return pltpu.CompilerParams(vmem_limit_bytes=size)


def pick_kernel(step, riding, *refs):
    three_c = refs[0]
    out, token, sems = refs[-3:]
    token[...] = jnp.zeros_like(token)
    _, count, _ = out.shape
    square = three_c.shape[2]
    pairs = [(three_c.at[lax.axis_index("ri") ^ step], out.at[0, :, pl.ds(0, square)])]
    if riding:
        coulomb = refs[1]
        rows, total = coulomb.shape
        fold = count // rows
        wide = total // fold
        for i in range(fold):
            there = out.at[0, pl.ds(i * rows, rows), pl.ds(square, wide)]
            pairs.append((coulomb.at[:, pl.ds(i * wide, wide)], there))
    finished(started(sems, pairs))


def pick(three_c, step, coulomb=None, hold=None):
    _, count, square = three_c.shape
    riding = coulomb is not None
    operands = [in_far(three_c)] + [in_far(a) for a in (coulomb,) if riding] + [a for a in (hold,) if a is not None]
    extra = coulomb.size // count if riding else 0
    rides = count // coulomb.shape[0] if riding else 0
    return pl.pallas_call(
        functools.partial(pick_kernel, step, riding),
        in_specs=[ANY] * (1 + riding) + [VMEM] * (hold is not None),
        out_specs=[VMEM, VMEM],
        out_shape=[near((1, count, square + extra)), half(TOKEN)],
        scratch_shapes=[pltpu.SemaphoreType.DMA((1 + rides,))],
        compiler_params=limit(SMALL_LIMIT),
        name="pick",
    )(*operands)


def along_x_kernel(block, coulomb, ids, hold, out):
    rows, total = coulomb.shape
    upper = (lax.axis_index("ri") & 2) != 0
    own = coulomb[...]
    fold = block.shape[1] // rows
    tail = block[0, :, block.shape[2] - total // fold :]
    other = jnp.concatenate([tail[i * rows : (i + 1) * rows] for i in range(fold)], 1)
    out[0, :rows, :total] = jnp.where(upper, other, own)
    out[0, rows:, :total] = jnp.where(upper, own, other)
    out[0, :, total:] = ids[...]


def rows_along_x(block, coulomb, ids, hold):
    rows, total = coulomb.shape
    return pl.pallas_call(
        along_x_kernel,
        in_specs=[VMEM] * 4,
        out_specs=VMEM,
        out_shape=half((1, 2 * rows, total + LANES)),
        compiler_params=limit(SMALL_LIMIT),
        name="rows_along_x",
    )(block, coulomb, ids, hold)


def prepared(size, occ, virt, occ_out, virt_out, back_out=None):
    width = occ.shape[0]
    full = occ_out.shape[0]
    spread = one(iota((full, width), 0) % width == iota((full, width), 1))
    tiled = dot_nt(dot(spread, occ).astype(jnp.bfloat16), spread)
    same = iota((full, full), 0) // width == iota((full, full), 1) // width
    occ_out[...] = jnp.where(same, tiled, 0.0).astype(jnp.bfloat16)

    keep = (iota((width, width), 0) < size) & (iota((width, width), 1) < size)
    kept = jnp.where(keep, virt.astype(jnp.float32), 0.0).astype(jnp.bfloat16)
    side = virt_out.shape[0] // 2
    same = iota((side, 2 * side), 0) % SUB == iota((side, 2 * side), 1) % SUB
    for parity in range(2):
        wanted = 2 * (iota((side, width), 0) // SUB) + parity
        picked_rows = one(wanted == iota((side, width), 1))
        column = iota((2 * side, width), 0)
        wanted = 2 * (column % side // SUB) + (column // side + parity) % 2
        picked_columns = one(wanted == iota((2 * side, width), 1))
        for target, product in ((virt_out, dot), (back_out, dot_nt)):
            if target is not None:
                part = dot_nt(product(picked_rows, kept).astype(jnp.bfloat16), picked_columns)
                target[parity * side : (parity + 1) * side, :] = jnp.where(same, part, 0.0).astype(jnp.bfloat16)


def times_occ(block, occ, left, product=dot):
    rows, square = left.shape
    full = occ.shape[0]
    wide = [block[:, c * full : (c + 1) * full] for c in range(square // full)]
    out = product(jnp.concatenate(wide, 0), occ[...]).astype(jnp.bfloat16)
    for c in range(square // full):
        left[:, c * full : (c + 1) * full] = out[c * rows : (c + 1) * rows]


def times_virt(virt, block, right):
    rows, square = right.shape
    chunks = square // LANES
    side = chunks * SUB
    low = iota((side, 2 * LANES), 1) % LANES < LANES // 2
    for row in range(0, rows, 2 * SUB):
        tile = block[row : row + 2 * SUB, :square].astype(jnp.float32)
        plain, turned = [], []
        for i in range(2):
            part = tile[i * SUB : (i + 1) * SUB]
            stacked = jnp.concatenate([part[:, c * LANES : (c + 1) * LANES] for c in range(chunks)], 0)
            plain.append(stacked)
            turned.append(pltpu.roll(stacked, LANES // 2, 1))
        operand = jnp.concatenate([jnp.concatenate(plain, 1), jnp.concatenate(turned, 1)], 0)
        out = dot(virt[...], operand.astype(jnp.bfloat16))
        out = jnp.where(low, out[:side], out[side:])
        for c in range(chunks):
            piece = out[c * SUB : (c + 1) * SUB]
            piece = jnp.concatenate([piece[:, :LANES], piece[:, LANES:]], 0)
            right[row : row + 2 * SUB, c * LANES : (c + 1) * LANES] = piece.astype(jnp.bfloat16)


def long_dot(lefts, rights, pad=0):
    square = lefts[0].shape[1]
    step = 1024
    total = None
    for c in range(0, square, step):
        a = jnp.concatenate([ref[:, c : c + step] for ref in lefts], 0)
        b = [ref[:, c : c + step] for ref in rights]
        zeros = [jnp.zeros((abs(pad), step), jnp.bfloat16)] if pad else []
        b = jnp.concatenate(b + zeros if pad > 0 else zeros + b, 0)
        part = dot_nt(a, b)
        total = part if total is None else total + part
    return total


def corner_kernel(step, sizes, three_c, occ, virt, hold, out, token, occ_wide, virt_wide, left, right, sem):
    token[...] = jnp.zeros_like(token)
    there = lax.axis_index("ri") ^ step
    rows, square = left.shape
    block = out.at[0, :, pl.ds(0, square)]
    copy = pltpu.make_async_copy(three_c.at[there], block, sem)
    copy.start()
    prepared(sizes[there], occ[there], virt[there], occ_wide, virt_wide)
    copy.wait()
    times_occ(block, occ_wide, left)
    times_virt(virt_wide, block, right)
    out[0, :, square:] = long_dot([left], [right], -rows).astype(jnp.bfloat16)


def corner(three_c, step, occ, virt, sizes, hold):
    _, rows, square = three_c.shape
    width = occ.shape[-1]
    shapes = [(4 * width, 4 * width), (SUB * width, SUB * width), (rows, square), (rows, square)]
    return pl.pallas_call(
        functools.partial(corner_kernel, step),
        in_specs=[SMEM, ANY, VMEM, VMEM, VMEM],
        out_specs=[VMEM, VMEM],
        out_shape=[near((1, rows, square + 2 * rows)), half(TOKEN)],
        scratch_shapes=[pltpu.VMEM(shape, jnp.bfloat16) for shape in shapes] + [pltpu.SemaphoreType.DMA],
        compiler_params=limit(VMEM_LIMIT),
        name="corner",
    )(sizes, in_far(three_c), occ, virt, hold)


def first_kernel(sizes, ids, three_c, other, occ, virt, hold, *refs):
    occ_out, virt_out, back_out, place, left, right, left_back, right_back, token, own, sem = refs
    token[...] = jnp.zeros_like(token)
    here = lax.axis_index("ri")
    copy = pltpu.make_async_copy(three_c.at[here], own, sem)
    copy.start()
    prepared(sizes[here], occ[here], virt[here], occ_out, virt_out, back_out)
    rows, square = own.shape
    column = iota(place.shape, 1)
    wanted = jnp.zeros(place.shape, jnp.int32)
    for j in range(ids.shape[1]):
        wanted = jnp.where(column // rows == j, ids[here, here ^ j], wanted)
    row = iota(place.shape, 0)
    place[...] = one((row // rows == wanted) & (row % rows == column % rows))
    copy.wait()
    for i, block in enumerate((own, other.at[0])):
        at = slice(i * rows, (i + 1) * rows)
        times_occ(block, occ_out, left.at[at])
        times_virt(virt_out, block, right.at[at])
        times_virt(back_out, left.at[at], left_back.at[at])
        times_occ(right.at[at], occ_out, right_back.at[at], dot_nt)


def first_blocks(three_c, other, occ, virt, sizes, ids, hold):
    _, rows, square = three_c.shape
    width = occ.shape[-1]
    kcount = ids.shape[1]
    shapes = [(4 * width, 4 * width)] + [(SUB * width, SUB * width)] * 2
    shapes += [(2 * kcount * rows, kcount * rows)] + [(2 * rows, square)] * 4
    return pl.pallas_call(
        first_kernel,
        in_specs=[SMEM, SMEM, ANY] + [VMEM] * 4,
        out_specs=[VMEM] * 9,
        out_shape=[near(shape) for shape in shapes] + [half(TOKEN)],
        scratch_shapes=[pltpu.VMEM((rows, square), jnp.bfloat16), pltpu.SemaphoreType.DMA],
        compiler_params=limit(VMEM_LIMIT),
        name="first_blocks",
    )(sizes, ids, in_far(three_c), other, occ, virt, hold)


def next_kernel(block, occ, virt, virt_back, hold, left, right, left_back, right_back, token):
    token[...] = jnp.zeros_like(token)
    times_occ(block.at[0], occ, left)
    times_virt(virt, block.at[0], right)
    times_virt(virt_back, left, left_back)
    times_occ(right, occ, right_back, dot_nt)


def next_block(block, occ, virt, virt_back, hold, square):
    shape = (block.shape[1], square)
    return pl.pallas_call(
        next_kernel,
        in_specs=[VMEM] * 5,
        out_specs=[VMEM] * 5,
        out_shape=[near(shape)] * 4 + [half(TOKEN)],
        compiler_params=limit(VMEM_LIMIT),
        name="next_block",
    )(block, *map(in_near, (occ, virt, virt_back)), hold)


def inner_kernel(count, *refs):
    out, token = refs[2 * count :]
    token[...] = jnp.zeros_like(token)
    out[...] = long_dot(refs[:count], refs[count : 2 * count], out.shape[1] - out.shape[0]).astype(jnp.bfloat16)


def inner_chi(lefts, rights):
    rows = sum(left.shape[0] for left in lefts)
    wide = rows + lefts[-1].shape[0]
    return pl.pallas_call(
        functools.partial(inner_kernel, len(lefts)),
        in_specs=[VMEM] * (2 * len(lefts)),
        out_specs=[VMEM, VMEM],
        out_shape=[near((rows, wide)), half(TOKEN)],
        compiler_params=limit(VMEM_LIMIT),
        name="inner_chi",
    )(*map(in_near, lefts + rights))


def last_kernel(count, block, place, inner, *refs):
    right_backs, left_backs, out = refs[:count], refs[count : 2 * count], refs[2 * count]
    square = left_backs[0].shape[1]
    rows = block.shape[1]
    came = block.at[0, :, pl.ds(0, square)]
    aside = jnp.zeros((rows, inner.shape[1] - 2 * rows), jnp.float32)
    bottom = long_dot([came], right_backs, rows)
    bottom = bottom + jnp.concatenate([aside, block[0, :, square:].astype(jnp.float32)], 1)
    columns = long_dot(left_backs, [came], -rows)
    head, tail = inner[:, : -2 * rows], inner[:, -2 * rows :]
    top = jnp.concatenate([head, tail + columns.astype(jnp.bfloat16)], 1)
    total = jnp.concatenate([top, bottom.astype(jnp.bfloat16)], 0)
    out[...] = dot(place[...], total).astype(jnp.bfloat16)


def last_block(block, place, inner, right_backs, left_backs):
    return pl.pallas_call(
        functools.partial(last_kernel, len(left_backs)),
        in_specs=[VMEM] * (3 + 2 * len(left_backs)),
        out_specs=VMEM,
        out_shape=half(place.shape),
        compiler_params=limit(VMEM_LIMIT),
        name="last_block",
    )(block, *map(in_near, (place, inner, *right_backs, *left_backs)))


def finish_kernel(kcount, place, got, metric, chi_out, screen_out, chi, screen, sems):
    rows, total = chi.shape
    blocks = 2 * kcount
    width = total // blocks
    group = place.shape[0] // (kcount * blocks)
    devices = got.shape[0] // rows
    low = iota((group, LANES), 1) < width
    for first in range(0, rows, group):
        part = got[...]
        if group < rows:
            part = jnp.concatenate([part[d * rows + first : d * rows + first + group] for d in range(devices)], 0)
        step = 2 * blocks * group
        placed = [
            dot(place[h * step : (h + 1) * step, :], part[:, h * LANES : (h + 1) * LANES]) for h in range(kcount // 2)
        ]

        def block(t):
            straight, turned = None, None
            for j in range(kcount):
                at = (j % 2 * blocks + t) * group
                piece = placed[j // 2][at : at + group]
                if j % 2 == t % 2:
                    straight = piece if straight is None else straight + piece
                else:
                    turned = piece if turned is None else turned + piece
            return straight + pltpu.roll(turned, width, 1)

        for t in range(0, blocks, 2):
            chi[first : first + group, t * width : (t + 2) * width] = jnp.where(low, block(t), block(t + 1))
    copies = started(sems, [(chi, chi_out)])
    screen[...] = dot(chi[...].astype(jnp.bfloat16), metric[...])
    copies.append(pltpu.make_async_copy(screen, screen_out, sems.at[1]))
    copies[-1].start()
    finished(copies)


def finish(place, got, metric, kcount, rows):
    shape = (rows, metric.shape[0])
    return pl.pallas_call(
        functools.partial(finish_kernel, kcount),
        in_specs=[VMEM] * 3,
        out_specs=[ANY, ANY],
        out_shape=[jax.ShapeDtypeStruct(shape, jnp.float32)] * 2,
        scratch_shapes=[pltpu.VMEM(shape, jnp.float32)] * 2 + [pltpu.SemaphoreType.DMA((2,))],
        compiler_params=limit(VMEM_LIMIT),
        name="finish",
    )(place, got, metric)


def placing_kernel(hits, out):
    high, wide = hits.shape
    rows = out.shape[0] // high
    down = one(iota((high * rows, high), 0) // rows == iota((high * rows, high), 1))
    across = one(iota((wide * rows, wide), 0) // rows == iota((wide * rows, wide), 1))
    spread = dot_nt(dot(down, hits[...]).astype(jnp.bfloat16), across)
    same = iota(out.shape, 0) % rows == iota(out.shape, 1) % rows
    out[...] = jnp.where(same, spread, 0.0).astype(jnp.bfloat16)


def placing(hits, rows):
    return pl.pallas_call(
        placing_kernel,
        in_specs=[VMEM],
        out_specs=VMEM,
        out_shape=half((hits.shape[0] * rows, hits.shape[1] * rows)),
        compiler_params=limit(VMEM_LIMIT),
        name="placing",
    )(hits)


def swap(array, axes, step):
    count = lax.axis_size(axes)
    return lax.ppermute(array, axes, [(i, i ^ step) for i in range(count)])


def join_kernel(axis, step, own, other, *refs):
    out = refs[-1]
    upper = (lax.axis_index(axis) & step) != 0
    out[0] = jnp.where(upper, other[...], own[...])
    out[1] = jnp.where(upper, own[...], other[...])


def gathered(array, axis, step, hold=None):
    other = swap(array, axis, step)
    return pl.pallas_call(
        functools.partial(join_kernel, axis, step),
        in_specs=[VMEM] * (2 + (hold is not None)),
        out_specs=VMEM,
        out_shape=half((2,) + array.shape),
        compiler_params=limit(SMALL_LIMIT),
        name="join",
    )(array, other, *([] if hold is None else [hold]))


def gather_metric(out, total, own_rows, pairs, kcount, hold):
    ri_count, pair_count = lax.axis_size("ri"), lax.axis_size("pair")
    chips = ri_count // 4
    _, rows, wide = out.shape
    step = 4
    while step < ri_count:
        out = gathered(out, "ri", step).reshape(-1, rows, wide)
        step *= 2
    step = pair_count // 2
    bits = 0
    while step:
        out = gathered(out, "pair", step, None if bits else hold).reshape(-1, rows, wide)
        step //= 2
        bits += 1
    back = tuple(reversed(range(bits)))
    all_ids = out.reshape((2,) * bits + (chips, rows, wide))[..., 0, :pairs, total : total + kcount]
    all_ids = all_ids.transpose(back + (bits, bits + 1)).reshape(-1, kcount)
    out = out[:, :, :total].reshape(-1, rows // 2, total)[:, :own_rows]
    out = gathered(out, "ri", 1).reshape((2,) + (2,) * bits + (2 * chips, own_rows, total))
    out = out.transpose(tuple(1 + bit for bit in back) + (bits + 1, 0, bits + 2, bits + 3))
    return out.reshape(-1, total), all_ids


def shards(three_c, green_occ, green_virt, pair_size, ri_ids, coulomb):
    everyone = ("pair", "ri")
    ri_count = lax.axis_size("ri")
    devices = lax.axis_size(everyone)
    kcount = ri_ids.shape[1]
    blocks = 2 * kcount
    pairs, _, rows, square = three_c.shape
    out_rows, total = coulomb.shape
    three_c = three_c.reshape(pairs, rows, square)
    slots = jnp.arange(kcount, dtype=jnp.int32)
    block_ids = jnp.arange(blocks, dtype=jnp.int32)
    riding_rows = max(16, out_rows)
    riding = jnp.pad(coulomb, ((0, riding_rows - out_rows), (0, 0)))

    parts, token = {}, None
    last = ri_count - 1
    for step in [2, 1] + list(range(3, last)):
        part, token = pick(three_c, step, coulomb=riding if step == 2 else None, hold=token)
        parts[step] = swap(part, "ri", step)
    part, token = corner(three_c, last, green_occ, green_virt, pair_size, token)
    parts[last] = swap(part, "ri", last)
    occ, virt, virt_back, place, left, right, left_back, right_back, token = first_blocks(
        three_c, parts[1], green_occ, green_virt, pair_size, ri_ids, token
    )
    lefts, rights, left_backs, right_backs = [left], [right], [left_back], [right_back]
    first_token = token
    for step in range(2, last):
        left, right, left_back, right_back, token = next_block(parts[step], occ, virt, virt_back, token, square)
        lefts.append(left)
        rights.append(right)
        left_backs.append(left_back)
        right_backs.append(right_back)
    inner, token = inner_chi(lefts, rights)
    pieces = last_block(parts[last], place, inner, right_backs, left_backs)

    slot = jnp.arange(pairs, dtype=jnp.int32)[:, None] ^ slots[None, :]
    relative = jnp.sum(jnp.where(slot[:, :, None] == slots, ri_ids[:, None, :], 0), 2)
    ids = jnp.pad(relative.astype(jnp.bfloat16), ((0, 2 * riding_rows - pairs), (0, LANES - kcount)))
    metric = rows_along_x(parts[2], riding, ids, first_token)
    metric, all_ids = gather_metric(metric, total, out_rows, pairs, kcount, token)
    hits = all_ids.T[:, None, :] == block_ids.astype(jnp.bfloat16)[None, :, None]
    placed = placing(hits.astype(jnp.bfloat16).reshape(kcount * blocks, devices), min(out_rows, 16))

    got = lax.all_to_all(pieces.reshape(devices, out_rows, kcount * rows), everyone, 0, 0, tiled=True)
    return tuple(finish(placed, got.reshape(devices * out_rows, kcount * rows), metric, kcount, out_rows))


def solution(mesh):
    placed = (
        P(("snap", "pair"), "ri", None, None),
        P(("snap", "pair"), None, None),
        P(("snap", "pair"), None, None),
        P(("snap", "pair")),
        P(("snap", "pair"), None),
        P(("snap", "pair", "ri"), None),
    )
    return jax.shard_map(
        shards,
        mesh=mesh,
        in_specs=placed,
        out_specs=(P(("snap", "pair", "ri"), None), P(("snap", "pair", "ri"), None)),
        check_vma=False,
    )
```

```python
import functools

import jax
import jax.numpy as jnp
from jax import lax
from jax.experimental import pallas as pl
from jax.experimental.pallas import tpu as pltpu
from jax.sharding import PartitionSpec as P

LANES = 128
SUB = 8
TOKEN = (16, 128)
VMEM_LIMIT = 20 * 1024 * 1024
SMALL_LIMIT = 4 * 1024 * 1024
VMEM = pl.BlockSpec(memory_space=pltpu.VMEM)
SMEM = pl.BlockSpec(memory_space=pltpu.SMEM)
ANY = pl.BlockSpec(memory_space=pl.ANY)


def iota(shape, dim):
    return lax.broadcasted_iota(jnp.int32, shape, dim)


def one(hit):
    return jnp.where(hit, 1.0, 0.0).astype(jnp.bfloat16)


def dot(a, b):
    return jnp.dot(a, b, preferred_element_type=jnp.float32)


def dot_nt(a, b):
    return lax.dot_general(a, b, (((1,), (1,)), ((), ())), preferred_element_type=jnp.float32)


def half(shape):
    return jax.ShapeDtypeStruct(shape, jnp.bfloat16)


def far(shape):
    return pltpu.HBM(shape, jnp.bfloat16)


def near(shape):
    return pltpu.VMEM(shape, jnp.bfloat16)


def in_near(array):
    return pltpu.with_memory_space_constraint(array, pltpu.VMEM)


def in_far(array):
    return pltpu.with_memory_space_constraint(array, pltpu.HBM)


def started(sems, pairs):
    copies = [pltpu.make_async_copy(a, b, sems.at[i]) for i, (a, b) in enumerate(pairs)]
    for copy in copies:
        copy.start()
    return copies


def finished(copies):
    for copy in copies:
        copy.wait()


def limit(size):
    return pltpu.CompilerParams(vmem_limit_bytes=size)


def pick_kernel(step, riding, *refs):
    three_c = refs[0]
    out, token, sems = refs[-3:]
    token[...] = jnp.zeros_like(token)
    _, count, _ = out.shape
    square = three_c.shape[2]
    pairs = [(three_c.at[lax.axis_index("ri") ^ step], out.at[0, :, pl.ds(0, square)])]
    if riding:
        coulomb = refs[1]
        rows, total = coulomb.shape
        fold = count // rows
        wide = total // fold
        for i in range(fold):
            there = out.at[0, pl.ds(i * rows, rows), pl.ds(square, wide)]
            pairs.append((coulomb.at[:, pl.ds(i * wide, wide)], there))
    finished(started(sems, pairs))


def pick(three_c, step, coulomb=None, hold=None):
    _, count, square = three_c.shape
    riding = coulomb is not None
    operands = [in_far(three_c)] + [in_far(a) for a in (coulomb,) if riding] + [a for a in (hold,) if a is not None]
    extra = coulomb.size // count if riding else 0
    rides = count // coulomb.shape[0] if riding else 0
    return pl.pallas_call(
        functools.partial(pick_kernel, step, riding),
        in_specs=[ANY] * (1 + riding) + [VMEM] * (hold is not None),
        out_specs=[VMEM, VMEM],
        out_shape=[near((1, count, square + extra)), half(TOKEN)],
        scratch_shapes=[pltpu.SemaphoreType.DMA((1 + rides,))],
        compiler_params=limit(SMALL_LIMIT),
        name="pick",
    )(*operands)


def along_x_kernel(block, coulomb, ids, hold, out):
    rows, total = coulomb.shape
    upper = (lax.axis_index("ri") & 2) != 0
    own = coulomb[...]
    fold = block.shape[1] // rows
    tail = block[0, :, block.shape[2] - total // fold :]
    other = jnp.concatenate([tail[i * rows : (i + 1) * rows] for i in range(fold)], 1)
    out[0, :rows, :total] = jnp.where(upper, other, own)
    out[0, rows:, :total] = jnp.where(upper, own, other)
    out[0, :, total:] = ids[...]


def rows_along_x(block, coulomb, ids, hold):
    rows, total = coulomb.shape
    return pl.pallas_call(
        along_x_kernel,
        in_specs=[VMEM] * 4,
        out_specs=VMEM,
        out_shape=half((1, 2 * rows, total + LANES)),
        compiler_params=limit(SMALL_LIMIT),
        name="rows_along_x",
    )(block, coulomb, ids, hold)


def prepared(size, occ, virt, occ_out, virt_out, back_out=None):
    width = occ.shape[0]
    full = occ_out.shape[0]
    spread = one(iota((full, width), 0) % width == iota((full, width), 1))
    tiled = dot_nt(dot(spread, occ).astype(jnp.bfloat16), spread)
    same = iota((full, full), 0) // width == iota((full, full), 1) // width
    occ_out[...] = jnp.where(same, tiled, 0.0).astype(jnp.bfloat16)

    keep = (iota((width, width), 0) < size) & (iota((width, width), 1) < size)
    kept = jnp.where(keep, virt.astype(jnp.float32), 0.0).astype(jnp.bfloat16)
    side = virt_out.shape[0] // 2
    same = iota((side, 2 * side), 0) % SUB == iota((side, 2 * side), 1) % SUB
    for parity in range(2):
        wanted = 2 * (iota((side, width), 0) // SUB) + parity
        picked_rows = one(wanted == iota((side, width), 1))
        column = iota((2 * side, width), 0)
        wanted = 2 * (column % side // SUB) + (column // side + parity) % 2
        picked_columns = one(wanted == iota((2 * side, width), 1))
        for target, product in ((virt_out, dot), (back_out, dot_nt)):
            if target is not None:
                part = dot_nt(product(picked_rows, kept).astype(jnp.bfloat16), picked_columns)
                target[parity * side : (parity + 1) * side, :] = jnp.where(same, part, 0.0).astype(jnp.bfloat16)


def times_occ(block, occ, left, product=dot):
    rows, square = left.shape
    full = occ.shape[0]
    wide = [block[:, c * full : (c + 1) * full] for c in range(square // full)]
    out = product(jnp.concatenate(wide, 0), occ[...]).astype(jnp.bfloat16)
    for c in range(square // full):
        left[:, c * full : (c + 1) * full] = out[c * rows : (c + 1) * rows]


def times_virt(virt, block, right):
    rows, square = right.shape
    chunks = square // LANES
    side = chunks * SUB
    low = iota((side, 2 * LANES), 1) % LANES < LANES // 2
    for row in range(0, rows, 2 * SUB):
        tile = block[row : row + 2 * SUB, :square].astype(jnp.float32)
        plain, turned = [], []
        for i in range(2):
            part = tile[i * SUB : (i + 1) * SUB]
            stacked = jnp.concatenate([part[:, c * LANES : (c + 1) * LANES] for c in range(chunks)], 0)
            plain.append(stacked)
            turned.append(pltpu.roll(stacked, LANES // 2, 1))
        operand = jnp.concatenate([jnp.concatenate(plain, 1), jnp.concatenate(turned, 1)], 0)
        out = dot(virt[...], operand.astype(jnp.bfloat16))
        out = jnp.where(low, out[:side], out[side:])
        for c in range(chunks):
            piece = out[c * SUB : (c + 1) * SUB]
            piece = jnp.concatenate([piece[:, :LANES], piece[:, LANES:]], 0)
            right[row : row + 2 * SUB, c * LANES : (c + 1) * LANES] = piece.astype(jnp.bfloat16)


def long_dot(lefts, rights, pad=0):
    square = lefts[0].shape[1]
    step = 1024
    total = None
    for c in range(0, square, step):
        a = jnp.concatenate([ref[:, c : c + step] for ref in lefts], 0)
        b = [ref[:, c : c + step] for ref in rights]
        zeros = [jnp.zeros((abs(pad), step), jnp.bfloat16)] if pad else []
        b = jnp.concatenate(b + zeros if pad > 0 else zeros + b, 0)
        part = dot_nt(a, b)
        total = part if total is None else total + part
    return total


def corner_kernel(step, sizes, three_c, occ, virt, hold, out, token, occ_wide, virt_wide, left, right, sem):
    token[...] = jnp.zeros_like(token)
    there = lax.axis_index("ri") ^ step
    rows, square = left.shape
    block = out.at[0, :, pl.ds(0, square)]
    copy = pltpu.make_async_copy(three_c.at[there], block, sem)
    copy.start()
    prepared(sizes[there], occ[there], virt[there], occ_wide, virt_wide)
    copy.wait()
    times_occ(block, occ_wide, left)
    times_virt(virt_wide, block, right)
    out[0, :, square:] = long_dot([left], [right], -rows).astype(jnp.bfloat16)


def corner(three_c, step, occ, virt, sizes, hold):
    _, rows, square = three_c.shape
    width = occ.shape[-1]
    shapes = [(4 * width, 4 * width), (SUB * width, SUB * width), (rows, square), (rows, square)]
    return pl.pallas_call(
        functools.partial(corner_kernel, step),
        in_specs=[SMEM, ANY, VMEM, VMEM, VMEM],
        out_specs=[VMEM, VMEM],
        out_shape=[near((1, rows, square + 2 * rows)), half(TOKEN)],
        scratch_shapes=[pltpu.VMEM(shape, jnp.bfloat16) for shape in shapes] + [pltpu.SemaphoreType.DMA],
        compiler_params=limit(VMEM_LIMIT),
        name="corner",
    )(sizes, in_far(three_c), occ, virt, hold)


def first_kernel(sizes, ids, three_c, other, occ, virt, hold, *refs):
    occ_out, virt_out, back_out, place, left, right, left_back, right_back, token, own, sem = refs
    token[...] = jnp.zeros_like(token)
    here = lax.axis_index("ri")
    copy = pltpu.make_async_copy(three_c.at[here], own, sem)
    copy.start()
    prepared(sizes[here], occ[here], virt[here], occ_out, virt_out, back_out)
    rows, square = own.shape
    column = iota(place.shape, 1)
    wanted = jnp.zeros(place.shape, jnp.int32)
    for j in range(ids.shape[1]):
        wanted = jnp.where(column // rows == j, ids[here, here ^ j], wanted)
    row = iota(place.shape, 0)
    place[...] = one((row // rows == wanted) & (row % rows == column % rows))
    copy.wait()
    for i, block in enumerate((own, other.at[0])):
        at = slice(i * rows, (i + 1) * rows)
        times_occ(block, occ_out, left.at[at])
        times_virt(virt_out, block, right.at[at])
        times_virt(back_out, left.at[at], left_back.at[at])
        times_occ(right.at[at], occ_out, right_back.at[at], dot_nt)


def first_blocks(three_c, other, occ, virt, sizes, ids, hold):
    _, rows, square = three_c.shape
    width = occ.shape[-1]
    kcount = ids.shape[1]
    shapes = [(4 * width, 4 * width)] + [(SUB * width, SUB * width)] * 2
    shapes += [(2 * kcount * rows, kcount * rows)] + [(2 * rows, square)] * 4
    return pl.pallas_call(
        first_kernel,
        in_specs=[SMEM, SMEM, ANY] + [VMEM] * 4,
        out_specs=[VMEM] * 9,
        out_shape=[near(shape) for shape in shapes] + [half(TOKEN)],
        scratch_shapes=[pltpu.VMEM((rows, square), jnp.bfloat16), pltpu.SemaphoreType.DMA],
        compiler_params=limit(VMEM_LIMIT),
        name="first_blocks",
    )(sizes, ids, in_far(three_c), other, occ, virt, hold)


def next_kernel(block, occ, virt, virt_back, hold, left, right, left_back, right_back, token):
    token[...] = jnp.zeros_like(token)
    times_occ(block.at[0], occ, left)
    times_virt(virt, block.at[0], right)
    times_virt(virt_back, left, left_back)
    times_occ(right, occ, right_back, dot_nt)


def next_block(block, occ, virt, virt_back, hold, square):
    shape = (block.shape[1], square)
    return pl.pallas_call(
        next_kernel,
        in_specs=[VMEM] * 5,
        out_specs=[VMEM] * 5,
        out_shape=[near(shape)] * 4 + [half(TOKEN)],
        compiler_params=limit(VMEM_LIMIT),
        name="next_block",
    )(block, *map(in_near, (occ, virt, virt_back)), hold)


def inner_kernel(count, *refs):
    out, token = refs[2 * count :]
    token[...] = jnp.zeros_like(token)
    out[...] = long_dot(refs[:count], refs[count : 2 * count], out.shape[1] - out.shape[0]).astype(jnp.bfloat16)


def inner_chi(lefts, rights):
    rows = sum(left.shape[0] for left in lefts)
    wide = rows + lefts[-1].shape[0]
    return pl.pallas_call(
        functools.partial(inner_kernel, len(lefts)),
        in_specs=[VMEM] * (2 * len(lefts)),
        out_specs=[VMEM, VMEM],
        out_shape=[near((rows, wide)), half(TOKEN)],
        compiler_params=limit(VMEM_LIMIT),
        name="inner_chi",
    )(*map(in_near, lefts + rights))


def last_kernel(count, block, place, inner, *refs):
    right_backs, left_backs, out = refs[:count], refs[count : 2 * count], refs[2 * count]
    square = left_backs[0].shape[1]
    rows = block.shape[1]
    came = block.at[0, :, pl.ds(0, square)]
    aside = jnp.zeros((rows, inner.shape[1] - 2 * rows), jnp.float32)
    bottom = long_dot([came], right_backs, rows)
    bottom = bottom + jnp.concatenate([aside, block[0, :, square:].astype(jnp.float32)], 1)
    columns = long_dot(left_backs, [came], -rows)
    head, tail = inner[:, : -2 * rows], inner[:, -2 * rows :]
    top = jnp.concatenate([head, tail + columns.astype(jnp.bfloat16)], 1)
    total = jnp.concatenate([top, bottom.astype(jnp.bfloat16)], 0)
    out[...] = dot(place[...], total).astype(jnp.bfloat16)


def last_block(block, place, inner, right_backs, left_backs):
    return pl.pallas_call(
        functools.partial(last_kernel, len(left_backs)),
        in_specs=[VMEM] * (3 + 2 * len(left_backs)),
        out_specs=VMEM,
        out_shape=half(place.shape),
        compiler_params=limit(VMEM_LIMIT),
        name="last_block",
    )(block, *map(in_near, (place, inner, *right_backs, *left_backs)))


def finish_kernel(kcount, place, got, metric, chi_out, screen_out, chi, screen, sems):
    rows, total = chi.shape
    blocks = 2 * kcount
    width = total // blocks
    group = place.shape[0] // (kcount * blocks)
    devices = got.shape[0] // rows
    low = iota((group, LANES), 1) < width
    for first in range(0, rows, group):
        part = got[...]
        if group < rows:
            part = jnp.concatenate([part[d * rows + first : d * rows + first + group] for d in range(devices)], 0)
        placed = dot(place[...], part)

        def block(t):
            straight, turned = None, None
            for j in range(kcount):
                at = (j * blocks + t) * group
                piece = placed[at : at + group, j // 2 * LANES : (j // 2 + 1) * LANES]
                if j % 2 == t % 2:
                    straight = piece if straight is None else straight + piece
                else:
                    turned = piece if turned is None else turned + piece
            return straight + pltpu.roll(turned, width, 1)

        for t in range(0, blocks, 2):
            chi[first : first + group, t * width : (t + 2) * width] = jnp.where(low, block(t), block(t + 1))
        ready = chi[first : first + group, :].astype(jnp.bfloat16)
        screen[first : first + group, :] = dot(ready, metric[...])
    copies = started(sems, [(chi, chi_out)])
    copies.append(pltpu.make_async_copy(screen, screen_out, sems.at[1]))
    copies[-1].start()
    finished(copies)


def finish(place, got, metric, kcount, rows):
    shape = (rows, metric.shape[0])
    return pl.pallas_call(
        functools.partial(finish_kernel, kcount),
        in_specs=[VMEM] * 3,
        out_specs=[ANY, ANY],
        out_shape=[jax.ShapeDtypeStruct(shape, jnp.float32)] * 2,
        scratch_shapes=[pltpu.VMEM(shape, jnp.float32)] * 2 + [pltpu.SemaphoreType.DMA((2,))],
        compiler_params=limit(VMEM_LIMIT),
        name="finish",
    )(place, got, metric)


def placing_kernel(hits, out):
    high, wide = hits.shape
    rows = out.shape[0] // high
    down = one(iota((high * rows, high), 0) // rows == iota((high * rows, high), 1))
    across = one(iota((wide * rows, wide), 0) // rows == iota((wide * rows, wide), 1))
    spread = dot_nt(dot(down, hits[...]).astype(jnp.bfloat16), across)
    same = iota(out.shape, 0) % rows == iota(out.shape, 1) % rows
    out[...] = jnp.where(same, spread, 0.0).astype(jnp.bfloat16)


def placing(hits, rows):
    return pl.pallas_call(
        placing_kernel,
        in_specs=[VMEM],
        out_specs=VMEM,
        out_shape=half((hits.shape[0] * rows, hits.shape[1] * rows)),
        compiler_params=limit(VMEM_LIMIT),
        name="placing",
    )(hits)


def swap(array, axes, step):
    count = lax.axis_size(axes)
    return lax.ppermute(array, axes, [(i, i ^ step) for i in range(count)])


def join_kernel(axis, step, own, other, *refs):
    out = refs[-1]
    upper = (lax.axis_index(axis) & step) != 0
    out[0] = jnp.where(upper, other[...], own[...])
    out[1] = jnp.where(upper, own[...], other[...])


def gathered(array, axis, step, hold=None):
    other = swap(array, axis, step)
    return pl.pallas_call(
        functools.partial(join_kernel, axis, step),
        in_specs=[VMEM] * (2 + (hold is not None)),
        out_specs=VMEM,
        out_shape=half((2,) + array.shape),
        compiler_params=limit(SMALL_LIMIT),
        name="join",
    )(array, other, *([] if hold is None else [hold]))


def gather_metric(out, total, own_rows, pairs, kcount, hold):
    ri_count, pair_count = lax.axis_size("ri"), lax.axis_size("pair")
    chips = ri_count // 4
    _, rows, wide = out.shape
    step = 4
    while step < ri_count:
        out = gathered(out, "ri", step).reshape(-1, rows, wide)
        step *= 2
    step = 1
    while step < pair_count:
        out = gathered(out, "pair", step, hold if step == 1 else None).reshape(-1, rows, wide)
        step *= 2
    all_ids = out.reshape(pair_count, chips, rows, wide)[:, 0, :pairs, total : total + kcount]
    out = out[:, :, :total].reshape(-1, rows // 2, total)[:, :own_rows]
    out = gathered(out, "ri", 1).swapaxes(0, 1).reshape(-1, total)
    return out, all_ids.reshape(-1, kcount)


def shards(three_c, green_occ, green_virt, pair_size, ri_ids, coulomb):
    everyone = ("pair", "ri")
    ri_count = lax.axis_size("ri")
    devices = lax.axis_size(everyone)
    kcount = ri_ids.shape[1]
    blocks = 2 * kcount
    pairs, _, rows, square = three_c.shape
    out_rows, total = coulomb.shape
    three_c = three_c.reshape(pairs, rows, square)
    slots = jnp.arange(kcount, dtype=jnp.int32)
    block_ids = jnp.arange(blocks, dtype=jnp.int32)
    riding_rows = max(16, out_rows)
    riding = jnp.pad(coulomb, ((0, riding_rows - out_rows), (0, 0)))

    parts, token = {}, None
    last = ri_count - 1
    for step in [2, 1] + list(range(3, last)):
        part, token = pick(three_c, step, coulomb=riding if step == 2 else None, hold=token)
        parts[step] = swap(part, "ri", step)
    part, token = corner(three_c, last, green_occ, green_virt, pair_size, token)
    parts[last] = swap(part, "ri", last)
    occ, virt, virt_back, place, left, right, left_back, right_back, token = first_blocks(
        three_c, parts[1], green_occ, green_virt, pair_size, ri_ids, token
    )
    lefts, rights, left_backs, right_backs = [left], [right], [left_back], [right_back]
    first_token = token
    for step in range(2, last):
        left, right, left_back, right_back, token = next_block(parts[step], occ, virt, virt_back, token, square)
        lefts.append(left)
        rights.append(right)
        left_backs.append(left_back)
        right_backs.append(right_back)
    inner, token = inner_chi(lefts, rights)
    pieces = last_block(parts[last], place, inner, right_backs, left_backs)

    slot = jnp.arange(pairs, dtype=jnp.int32)[:, None] ^ slots[None, :]
    relative = jnp.sum(jnp.where(slot[:, :, None] == slots, ri_ids[:, None, :], 0), 2)
    ids = jnp.pad(relative.astype(jnp.bfloat16), ((0, 2 * riding_rows - pairs), (0, LANES - kcount)))
    metric = rows_along_x(parts[2], riding, ids, first_token)
    metric, all_ids = gather_metric(metric, total, out_rows, pairs, kcount, token)
    hits = all_ids.T[:, None, :] == block_ids.astype(jnp.bfloat16)[None, :, None]
    placed = placing(hits.astype(jnp.bfloat16).reshape(kcount * blocks, devices), min(out_rows, 16))

    got = lax.all_to_all(pieces.reshape(devices, out_rows, kcount * rows), everyone, 0, 0, tiled=True)
    return tuple(finish(placed, got.reshape(devices * out_rows, kcount * rows), metric, kcount, out_rows))


def solution(mesh):
    placed = (
        P(("snap", "pair"), "ri", None, None),
        P(("snap", "pair"), None, None),
        P(("snap", "pair"), None, None),
        P(("snap", "pair")),
        P(("snap", "pair"), None),
        P(("snap", "pair", "ri"), None),
    )
    return jax.shard_map(
        shards,
        mesh=mesh,
        in_specs=placed,
        out_specs=(P(("snap", "pair", "ri"), None), P(("snap", "pair", "ri"), None)),
        check_vma=False,
    )
```
